512 devices in a mesh: rep: 64 (over z, y_lo, core), fsdp: 8 (over x, y_hi).
Axes of the slice: x: 4, y: 8 (y_hi: 2, y_lo: 4; y = y_hi * 4 + y_lo), z: 8, core: 2. Of those that a mesh axis runs over, the one named last changes fastest.
Arguments:
- tokens: bfloat16 [65536, 4096], P(('rep', 'fsdp')), may hold values from -18 to 18
- targets: bfloat16 [65536, 1024], P(('rep', 'fsdp')), may hold values from -6 to 6
- local_weights: bfloat16 [64, 4096, 1024], P('rep', 'fsdp'), may hold values from -6 to 6
- pending_delta: bfloat16 [64, 4096, 256], P('rep', 'fsdp'), may hold values from -15 to 15
- frag_order: int32 [8], replicated, may hold values from 0 to 7, each once
- global_frag: bfloat16 [4096, 256], P('fsdp'), may hold values from -6 to 6
- outer_momentum: float32 [4096, 256], P('fsdp'), may hold values from -3 to 3
Outputs:
- new_weights: bfloat16 [64, 4096, 1024], P('rep', 'fsdp')
- new_global: bfloat16 [4096, 256], P('fsdp')
- new_momentum: float32 [4096, 256], P('fsdp')
The draws below stay inside these ranges and needn't reach their ends.
Inputs may be any that keep to these rules, and one draw needn't show every extreme that they name: frag_order is a permutation of 0 to 7; the pending fragment is made of heads frag_order[0] and frag_order[1].
All inputs are finite; a program needn't handle non-finite values.
Results may differ from the reference program's by a relative error of at most 0.0031.
Values may be sent and summed in bfloat16 or wider, within the bound.
No kernel may reach another device: no remote copies, remote signals or barrier semaphores. Data moves between devices by JAX's collectives and lax.ppermute only.
A program may use at most 64 MiB of HBM per device.

```python
import math
import jax
import jax.numpy as jnp
from jax import lax

D = 4096
KV_HEADS = 8
HEAD = 128
FRAG_HEADS = 2
KV = 1024
FRAG = 256
REPLICAS = 64
TOK_REP = 1024
TOKENS = 65536
N_REP = 64


def draw_tokens(key, part):
    key = jax.random.fold_in(key, 11)
    ramp = jnp.arange(D, dtype=jnp.float32) / (D - 1)
    base = jnp.clip(jax.random.normal(key, (TOKENS, D), jnp.float32), -6.0, 6.0)
    scale = jnp.exp(ramp * math.log(3.0))
    return (base * scale[None, :]).astype(jnp.bfloat16)


def levels(key, dims, shards, low, high):
    gain = 1.0
    for position, blocks in shards:
        heights = jax.random.uniform(jax.random.fold_in(jax.random.fold_in(key, 6), position), (blocks,), jnp.float32, low / len(shards), high / len(shards))
        gain = gain * jnp.repeat(jnp.exp(heights), dims[position] // blocks).reshape((-1,) + (1,) * (len(dims) - 1 - position))
    return gain


def noise(key, extent, width, limit, shards=(), kind=jnp.bfloat16):
    gain = levels(key, extent, shards, -0.22, 0.18) if shards else 1.0
    entries = jax.random.normal(key, extent, jnp.float32) * width * gain
    return jnp.minimum(jnp.maximum(entries, -limit), limit).astype(kind)


def setup_inputs(seed: int = 0) -> dict:
    splits = jax.random.split(jax.random.key(seed), 8)
    tokens = draw_tokens(jax.random.fold_in(splits[7], 71), 0)
    targets = noise(splits[1], (TOKENS, KV), 1.0, 6.0, ((0, 512),))
    local_weights = noise(splits[2], (REPLICAS, D, KV), 1.0, 6.0, ((0, 64), (1, 8)))
    pending_delta = noise(splits[3], (REPLICAS, D, FRAG), 2.5, 15.0, ((0, 64), (1, 8)))
    frag_order = jax.random.permutation(splits[4], KV_HEADS).astype(jnp.int32)
    global_frag = noise(splits[5], (D, FRAG), 1.0, 6.0, ((0, 8),))
    outer_momentum = noise(splits[6], (D, FRAG), 0.5, 3.0, ((0, 8),), jnp.float32)
    return {"tokens": tokens, "targets": targets, "local_weights": local_weights, "pending_delta": pending_delta, "frag_order": frag_order, "global_frag": global_frag, "outer_momentum": outer_momentum}


def normalize(activations):
    floated = activations.astype(jnp.float32)
    meansq = lax.optimization_barrier(jnp.mean(floated * floated, axis=-1, keepdims=True))
    return (floated * lax.rsqrt(meansq + 1e-06)).astype(jnp.bfloat16)

def merge_fragment(stepped, new_global, frag_order):
    merged = stepped
    anchor = jnp.zeros((), jnp.int32)
    for head_slot in range(FRAG_HEADS):
        column = (frag_order[head_slot] * HEAD).astype(jnp.int32)
        current = lax.dynamic_slice(merged, (anchor, column), (merged.shape[0], HEAD))
        incoming = new_global[:, head_slot * HEAD:(head_slot + 1) * HEAD].astype(jnp.float32)
        blended = 0.5 * current + 0.5 * incoming
        merged = lax.dynamic_update_slice(merged, blended, (anchor, column))
    return merged.astype(jnp.bfloat16)

def reference(tokens, targets, local_weights, pending_delta, frag_order, global_frag, outer_momentum):
    factor = 1.0 / math.sqrt(D)
    delta_mean = lax.optimization_barrier(jnp.sum(pending_delta.astype(jnp.float32), axis=0)) / N_REP
    new_momentum = 0.9 * outer_momentum + delta_mean
    new_global = (global_frag.astype(jnp.float32) - 0.7 * (delta_mean + 0.9 * new_momentum)).astype(jnp.bfloat16)
    grouped_tokens = tokens.reshape(N_REP, TOK_REP, D)
    grouped_targets = targets.reshape(N_REP, TOK_REP, KV)

    def replica_round(inputs):
        replica_tokens, replica_targets, weight = inputs
        normed = normalize(replica_tokens)
        keys = jnp.dot(normed, weight, preferred_element_type=jnp.float32) * factor
        residual = (keys - replica_targets.astype(jnp.float32)).astype(jnp.bfloat16)
        gradient = jnp.dot(normed.T, residual, preferred_element_type=jnp.float32) * factor
        grad_scale = jnp.sqrt(jnp.sum(gradient * gradient) / (D * KV) + 1e-06)
        stepped = weight.astype(jnp.float32) - 0.25 * gradient / grad_scale
        return merge_fragment(stepped, new_global, frag_order)
    new_weights = lax.map(replica_round, (grouped_tokens, grouped_targets, local_weights))
    return (new_weights, new_global, new_momentum)
```

```python
import math

import jax
import jax.numpy as jnp
from jax import lax
from jax.sharding import PartitionSpec as P

D = 4096
HEAD = 128
FRAG_HEADS = 2
KV = 1024
NX = 4
COLS = KV // NX
F32 = jnp.float32
BF16 = jnp.bfloat16

X_GROUPS = [[x * 2 + h for x in range(NX)] for h in range(2)]
Z_GROUPS = [[z * 8 + l for z in range(8)] for l in range(8)]
L_GROUPS = [[z * 8 + l for l in range(8)] for z in range(8)]
SWAP = [(i, i ^ 1) for i in range(8)]


def exchange(blocks, axis, groups):
    return lax.all_to_all(blocks, axis, 0, 0, axis_index_groups=groups, tiled=True)


def share(block, axis, groups):
    count = len(groups[0]) if groups else 8
    return exchange(jnp.broadcast_to(block[None], (count, *block.shape)), axis, groups)


def swap(block):
    return lax.ppermute(block, "fsdp", SWAP)


def sum_over_rep(delta):
    by_z = exchange(delta.reshape(8, 64, 256), "rep", Z_GROUPS)
    part = jnp.sum(by_z.astype(F32), axis=0)
    by_l = exchange(part.reshape(8, 8, 256), "rep", L_GROUPS)
    total = jnp.sum(by_l, axis=0)
    rows = share(total, "rep", L_GROUPS).reshape(64, 256)
    return share(rows, "rep", Z_GROUPS).reshape(512, 256)


def body(tokens, targets, local_weights, pending_delta, frag_order, global_frag, outer_momentum):
    factor = 1.0 / math.sqrt(D)
    half = lax.axis_index("fsdp") % 2
    weight = local_weights[0]

    with jax.named_scope("weight_columns"):
        rows = jnp.concatenate([weight, targets], axis=0)
        blocks = rows.reshape(640, NX, COLS).transpose(1, 0, 2)
        columns = exchange(blocks, "fsdp", X_GROUPS)
        my_weight = columns[:, :512].reshape(2048, COLS)
        my_targets = columns[:, 512:].reshape(512, COLS)

    with jax.named_scope("normalize"):
        floated = tokens.astype(F32)
        scale = lax.rsqrt(jnp.mean(floated * floated, axis=-1, keepdims=True) + 1e-06)
        normed = (floated * scale).astype(BF16).reshape(128, NX, 2, 512)
        mine = lax.dynamic_index_in_dim(normed, half, 2, keepdims=False).reshape(128, 2048)
        other = lax.dynamic_index_in_dim(normed, 1 - half, 2, keepdims=False).reshape(128, 2048)

    with jax.named_scope("activations"):
        arrived = swap(other)
        near = share(mine, "fsdp", X_GROUPS).reshape(512, 2048)
        far = share(arrived, "fsdp", X_GROUPS).reshape(512, 2048)

    with jax.named_scope("keys"):
        near_keys = jnp.dot(near, my_weight, preferred_element_type=F32) * factor
        near_part = near_keys - my_targets.astype(F32)
        far_rest = swap(near_part.astype(BF16))
        far_keys = jnp.dot(far, my_weight, preferred_element_type=F32) * factor
        near_rest = swap(far_keys.astype(BF16))
        far_residual = (far_keys + far_rest.astype(F32)).astype(BF16)
        near_residual = (near_part + near_rest.astype(F32)).astype(BF16)

    with jax.named_scope("gradient"):
        dims = (((0,), (0,)), ((), ()))
        gradient = (
            lax.dot_general(far, far_residual, dims, preferred_element_type=F32)
            + lax.dot_general(near, near_residual, dims, preferred_element_type=F32)
        ) * factor
        squares = jnp.sum(gradient * gradient)
        everyone = share(jnp.full((8, 128), squares, F32), "fsdp", None)
        total = jnp.sum(everyone[:, 0, 0])
        grad_scale = jnp.sqrt(total / (D * KV) + 1e-06)
        by_rows = exchange(gradient.astype(BF16).reshape(NX, 512, COLS), "fsdp", X_GROUPS)

    with jax.named_scope("outer"):
        delta_mean = sum_over_rep(pending_delta[0]) / lax.axis_size("rep")
        new_momentum = 0.9 * outer_momentum + delta_mean
        new_global = (
            global_frag.astype(F32) - 0.7 * (delta_mean + 0.9 * new_momentum)
        ).astype(BF16)

    with jax.named_scope("step"):
        row_gradient = by_rows.transpose(1, 0, 2).reshape(512, KV).astype(F32)
        merged = weight.astype(F32) - row_gradient * (0.25 / grad_scale)
        for slot in range(FRAG_HEADS):
            column = frag_order[slot] * HEAD
            current = lax.dynamic_slice(merged, (0, column), (512, HEAD))
            incoming = new_global[:, slot * HEAD : (slot + 1) * HEAD].astype(F32)
            merged = lax.dynamic_update_slice(
                merged, 0.5 * current + 0.5 * incoming, (0, column)
            )
        merged = merged.astype(BF16)
    return (merged[None], new_global, new_momentum)


def solution(mesh):
    placed = (
        P(("rep", "fsdp"), None),
        P(("rep", "fsdp"), None),
        P("rep", "fsdp", None),
        P("rep", "fsdp", None),
        P(),
        P("fsdp", None),
        P("fsdp", None),
    )
    return jax.shard_map(
        body,
        mesh=mesh,
        in_specs=placed,
        out_specs=(P("rep", "fsdp", None), P("fsdp", None), P("fsdp", None)),
        check_vma=False,
    )
```

```python
import functools
import math

import jax
import jax.numpy as jnp
from jax import lax
from jax.experimental import pallas as pl
from jax.experimental.pallas import tpu as pltpu
from jax.sharding import PartitionSpec as P

D = 4096
HEAD = 128
FRAG_HEADS = 2
KV = 1024
NX = 4
COLS = KV // NX
FACTOR = 1.0 / math.sqrt(D)
F32 = jnp.float32
BF16 = jnp.bfloat16
SDS = jax.ShapeDtypeStruct
SMEM = pl.BlockSpec(memory_space=pltpu.SMEM)
PARAMS = pltpu.CompilerParams(vmem_limit_bytes=40 * 1024 * 1024)

X_GROUPS = [[x * 2 + h for x in range(NX)] for h in range(2)]
Z_GROUPS = [[z * 8 + l for z in range(8)] for l in range(8)]
L_GROUPS = [[z * 8 + l for l in range(8)] for z in range(8)]


def exchange(blocks, axis, groups):
    return lax.all_to_all(blocks, axis, 0, 0, axis_index_groups=groups, tiled=True)


def share(block, groups):
    return exchange(jnp.broadcast_to(block[None], (8, *block.shape)), "rep", groups)


def flip(block, mask):
    return lax.ppermute(block, "fsdp", [(i, i ^ mask) for i in range(8)])


def rotate(blocks):
    moves = [[(x * 2 + h, (x + d) % NX * 2 + h) for x in range(NX) for h in range(2)] for d in range(NX)]
    return [blocks[0]] + [lax.ppermute(blocks[d], "fsdp", moves[d]) for d in (1, 2, 3)]


def gather(block):
    return rotate([block] * NX)


def after(value, earlier):
    return lax.optimization_barrier((value, earlier))[0]


def split_kernel(half_ref, tokens_ref, mine_ref, other_ref):
    half = half_ref[0]
    floated = tokens_ref[...].astype(F32)
    scale = lax.rsqrt(jnp.mean(floated * floated, axis=-1, keepdims=True) + 1e-06)
    for x in range(NX):
        for ref, side in ((mine_ref, half), (other_ref, 1 - half)):
            start = pl.multiple_of((2 * x + side) * 512, 512)
            piece = tokens_ref[:, pl.ds(start, 512)].astype(F32) * scale
            ref[:, x * 512 : (x + 1) * 512] = piece.astype(BF16)


def split(half, tokens):
    return pl.pallas_call(
        split_kernel,
        grid=(4,),
        in_specs=[SMEM, pl.BlockSpec((32, D), lambda i: (i, 0))],
        out_specs=[pl.BlockSpec((32, D // 2), lambda i: (i, 0))] * 2,
        out_shape=[SDS((128, D // 2), BF16)] * 2,
        compiler_params=PARAMS,
        name="split",
    )(half, tokens)


def pack_kernel(weight_ref, targets_ref, out_ref):
    for x in range(NX):
        columns = slice(x * COLS, (x + 1) * COLS)
        out_ref[x, :512] = weight_ref[0, :, columns]
        out_ref[x, 512:] = targets_ref[:, columns]


def raw_keys(blocks, columns_ref):
    lhs = jnp.concatenate([b[...] for b in blocks], axis=0)
    weight = columns_ref[:, :512, :].reshape(2048, COLS)
    return jnp.dot(lhs, weight, preferred_element_type=F32) * FACTOR


def near_kernel(x_ref, b0, b1, b2, b3, columns_ref, part_ref, sent_ref):
    keys = raw_keys((b0, b1, b2, b3), columns_ref)
    for d in range(NX):
        rows = slice(d * 128, (d + 1) * 128)
        source = lax.rem(x_ref[0] - d + NX, NX)
        part = keys[rows] - columns_ref[source, 512:, :].astype(F32)
        part_ref[rows] = part
        sent_ref[rows] = part.astype(BF16)


def far_kernel(b0, b1, b2, b3, columns_ref, rest_ref, sent_ref, residual_ref):
    keys = raw_keys((b0, b1, b2, b3), columns_ref)
    sent_ref[...] = keys.astype(BF16)
    residual_ref[...] = (keys + rest_ref[...].astype(F32)).astype(BF16)


def turn_kernel(b0, b1, b2, b3, out_ref):
    for d, b in enumerate((b0, b1, b2, b3)):
        out_ref[:, d * 128 : (d + 1) * 128] = b[...].T


def far_gradient_kernel(turned_ref, residual_ref, out_ref):
    out_ref[...] = jnp.dot(turned_ref[...], residual_ref[...], preferred_element_type=F32)


def near_gradient_kernel(turned_ref, part_ref, rest_ref, far_ref, out_ref, squares_ref):
    residual = (part_ref[...] + rest_ref[...].astype(F32)).astype(BF16)
    squares = jnp.zeros((8, COLS), F32)
    for x in range(NX):
        rows = slice(x * 512, (x + 1) * 512)
        near = jnp.dot(turned_ref[rows], residual, preferred_element_type=F32)
        gradient = (near + far_ref[rows]) * FACTOR
        out_ref[x] = gradient.astype(BF16)
        squares += jnp.sum((gradient * gradient).reshape(64, 8, COLS), axis=0)
    squares_ref[...] = squares[:, :128] + squares[:, 128:]


def step_kernel(order_ref, squares_ref, rows_ref, weight_ref, global_ref, out_ref, new_ref):
    total = jnp.sum(squares_ref[...], axis=(0, 1), keepdims=True)
    rate = 0.25 * lax.rsqrt(total / (D * KV) + 1e-06)
    for x in range(NX):
        columns = slice(x * COLS, (x + 1) * COLS)
        weight = weight_ref[0, :, columns].astype(F32)
        new_ref[:, columns] = weight - rows_ref[x].astype(F32) * rate
    for slot in range(FRAG_HEADS):
        at = pl.ds(pl.multiple_of(order_ref[slot] * HEAD, HEAD), HEAD)
        incoming = global_ref[:, slot * HEAD : (slot + 1) * HEAD].astype(F32)
        new_ref[:, at] = 0.5 * new_ref[:, at] + 0.5 * incoming
    out_ref[0] = new_ref[...].astype(BF16)


def step(order, squares, rows, weight, new_global):
    return pl.pallas_call(
        step_kernel,
        grid=(4,),
        in_specs=[
            SMEM,
            pl.BlockSpec((8, 128), lambda i: (0, 0)),
            pl.BlockSpec((NX, 128, COLS), lambda i: (0, i, 0)),
            pl.BlockSpec((1, 128, KV), lambda i: (0, i, 0)),
            pl.BlockSpec((128, COLS), lambda i: (i, 0)),
        ],
        out_specs=pl.BlockSpec((1, 128, KV), lambda i: (0, i, 0)),
        out_shape=SDS((1, 512, KV), BF16),
        scratch_shapes=[pltpu.VMEM((128, KV), F32)],
        compiler_params=PARAMS,
        name="step",
    )(order, squares, rows, weight, new_global)


def call(kernel, outs, *args, scalars=0, flops=0):
    return pl.pallas_call(
        kernel,
        in_specs=[SMEM] * scalars + [pl.BlockSpec(memory_space=pltpu.VMEM)] * (len(args) - scalars),
        out_specs=jax.tree.map(lambda _: pl.BlockSpec(memory_space=pltpu.VMEM), outs),
        out_shape=outs,
        compiler_params=PARAMS,
        cost_estimate=pl.CostEstimate(flops=flops, bytes_accessed=4 << 20, transcendentals=0),
        name=kernel.__name__.removesuffix("_kernel"),
    )(*args)


def body(tokens, targets, local_weights, pending_delta, frag_order, global_frag, outer_momentum):
    place = lax.axis_index("fsdp")
    half = lax.rem(place, 2).astype(jnp.int32).reshape(1)
    my_x = lax.div(place, 2).astype(jnp.int32).reshape(1)
    dot_flops = 2 * 512 * 2048 * COLS

    with jax.named_scope("activations"):
        mine, other = split(half, tokens)
        arrived = flip(other, 1)
        near = gather(mine)

    with jax.named_scope("weight_columns"):
        blocks = call(pack_kernel, SDS((NX, 640, COLS), BF16), local_weights, targets)
        columns = exchange(blocks, "fsdp", X_GROUPS)

    with jax.named_scope("far_activations"):
        far = gather(arrived)

    with jax.named_scope("keys"):
        tall = (512, COLS)
        near_part, near_sent = call(
            near_kernel, (SDS(tall, F32), SDS(tall, BF16)), my_x, *near, columns, scalars=1, flops=dot_flops
        )
        far_rest = flip(near_sent, 1)
        near_turned = call(turn_kernel, SDS((2048, 512), BF16), *near)
        far_turned = call(turn_kernel, SDS((2048, 512), BF16), *far)
        far_sent, far_residual = call(
            far_kernel, (SDS(tall, BF16), SDS(tall, BF16)), *far, columns, far_rest, flops=dot_flops
        )
        near_rest = flip(far_sent, 1)

    with jax.named_scope("outer_sum"):
        by_z = exchange(pending_delta[0].reshape(8, 64, 256), "rep", Z_GROUPS)
        part = jnp.sum(by_z.astype(F32), axis=0)
        by_l = share(part.astype(BF16), L_GROUPS)
        total = jnp.sum(by_l.astype(F32), axis=0)
        mean = share(total, Z_GROUPS).reshape(512, 256) / lax.axis_size("rep")
        new_momentum = 0.9 * outer_momentum + mean
        new_global = (global_frag.astype(F32) - 0.7 * (mean + 0.9 * new_momentum)).astype(BF16)

    with jax.named_scope("gradient"):
        far_gradient = call(
            far_gradient_kernel, SDS((2048, COLS), F32), far_turned, far_residual, flops=dot_flops
        )
        gradient, squares = call(
            near_gradient_kernel,
            (SDS((NX, 512, COLS), BF16), SDS((8, 128), F32)),
            near_turned, near_part, near_rest, far_gradient, flops=dot_flops,
        )
        by_rows = exchange(gradient, "fsdp", X_GROUPS)
        for mask in (2, 4, 1):
            squares = squares + flip(squares, mask)

    with jax.named_scope("step"):
        new_weights = step(frag_order, squares, by_rows, local_weights, new_global)
    return (new_weights, new_global, new_momentum)


def solution(mesh):
    placed = (
        P(("rep", "fsdp"), None),
        P(("rep", "fsdp"), None),
        P("rep", "fsdp", None),
        P("rep", "fsdp", None),
        P(),
        P("fsdp", None),
        P("fsdp", None),
    )
    return jax.shard_map(
        body,
        mesh=mesh,
        in_specs=placed,
        out_specs=(P("rep", "fsdp", None), P("fsdp", None), P("fsdp", None)),
        check_vma=False,
    )
```

```python
import math

import jax
import jax.numpy as jnp
from jax import lax
from jax.experimental import pallas as pl
from jax.experimental.pallas import tpu as pltpu
from jax.sharding import PartitionSpec as P

D = 4096
HEAD = 128
FRAG_HEADS = 2
KV = 1024
NX = 4
COLS = KV // NX
FACTOR = 1.0 / math.sqrt(D)
F32 = jnp.float32
BF16 = jnp.bfloat16
SDS = jax.ShapeDtypeStruct
SMEM = pl.BlockSpec(memory_space=pltpu.SMEM)
PARAMS = pltpu.CompilerParams(vmem_limit_bytes=40 * 1024 * 1024)

X_GROUPS = [[x * 2 + h for x in range(NX)] for h in range(2)]
Z_GROUPS = [[z * 8 + l for z in range(8)] for l in range(8)]
L_GROUPS = [[z * 8 + l for l in range(8)] for z in range(8)]


def exchange(blocks, axis, groups):
    return lax.all_to_all(blocks, axis, 0, 0, axis_index_groups=groups, tiled=True)


def flip(block, mask):
    return lax.ppermute(block, "fsdp", [(i, i ^ mask) for i in range(8)])


def rotate(blocks):
    moves = [[(x * 2 + h, (x + d) % NX * 2 + h) for x in range(NX) for h in range(2)] for d in range(NX)]
    return [blocks[0]] + [lax.ppermute(blocks[d], "fsdp", moves[d]) for d in (1, 2, 3)]


def gather(block):
    return rotate([block] * NX)


def split_kernel(half_ref, tokens_ref, mine_ref, other_ref):
    half = half_ref[0]
    floated = tokens_ref[...].astype(F32)
    scale = lax.rsqrt(jnp.mean(floated * floated, axis=-1, keepdims=True) + 1e-06)
    for x in range(NX):
        for ref, side in ((mine_ref, half), (other_ref, 1 - half)):
            start = pl.multiple_of((2 * x + side) * 512, 512)
            piece = tokens_ref[:, pl.ds(start, 512)].astype(F32) * scale
            ref[:, x * 512 : (x + 1) * 512] = piece.astype(BF16)


def split(half, tokens):
    return pl.pallas_call(
        split_kernel,
        grid=(4,),
        in_specs=[SMEM, pl.BlockSpec((32, D), lambda i: (i, 0))],
        out_specs=[pl.BlockSpec((32, D // 2), lambda i: (i, 0))] * 2,
        out_shape=[SDS((128, D // 2), BF16)] * 2,
        compiler_params=PARAMS,
        name="split",
    )(half, tokens)


def pack_kernel(weight_ref, targets_ref, out_ref):
    for x in range(NX):
        columns = slice(x * COLS, (x + 1) * COLS)
        out_ref[x, :512] = weight_ref[0, :, columns]
        out_ref[x, 512:] = targets_ref[:, columns]


def raw_keys(blocks, columns_ref):
    lhs = jnp.concatenate([b[...] for b in blocks], axis=0)
    weight = columns_ref[:, :512, :].reshape(2048, COLS)
    return jnp.dot(lhs, weight, preferred_element_type=F32) * FACTOR


def near_kernel(x_ref, b0, b1, b2, b3, columns_ref, part_ref, sent_ref):
    keys = raw_keys((b0, b1, b2, b3), columns_ref)
    for d in range(NX):
        rows = slice(d * 128, (d + 1) * 128)
        source = lax.rem(x_ref[0] - d + NX, NX)
        part = keys[rows] - columns_ref[source, 512:, :].astype(F32)
        part_ref[rows] = part
        sent_ref[rows] = part.astype(BF16)


def far_kernel(b0, b1, b2, b3, columns_ref, rest_ref, sent_ref, residual_ref):
    keys = raw_keys((b0, b1, b2, b3), columns_ref)
    sent_ref[...] = keys.astype(BF16)
    residual_ref[...] = (keys + rest_ref[...].astype(F32)).astype(BF16)


def turn_kernel(b0, b1, b2, b3, out_ref):
    for d, b in enumerate((b0, b1, b2, b3)):
        out_ref[:, d * 128 : (d + 1) * 128] = b[...].T


def far_gradient_kernel(turned_ref, residual_ref, out_ref):
    out_ref[...] = jnp.dot(turned_ref[...], residual_ref[...], preferred_element_type=F32)


def near_gradient_kernel(turned_ref, part_ref, rest_ref, far_ref, out_ref, squares_ref):
    residual = (part_ref[...] + rest_ref[...].astype(F32)).astype(BF16)
    squares = jnp.zeros((8, COLS), F32)
    for x in range(NX):
        rows = slice(x * 512, (x + 1) * 512)
        near = jnp.dot(turned_ref[rows], residual, preferred_element_type=F32)
        gradient = (near + far_ref[rows]) * FACTOR
        out_ref[x] = gradient.astype(BF16)
        squares += jnp.sum((gradient * gradient).reshape(64, 8, COLS), axis=0)
    squares_ref[...] = squares[:, :128] + squares[:, 128:]


def step_kernel(order_ref, squares_ref, rows_ref, weight_ref, global_ref, out_ref, new_ref):
    total = jnp.sum(squares_ref[...], axis=(0, 1), keepdims=True)
    rate = 0.25 * lax.rsqrt(total / (D * KV) + 1e-06)
    for x in range(NX):
        columns = slice(x * COLS, (x + 1) * COLS)
        weight = weight_ref[0, :, columns].astype(F32)
        new_ref[:, columns] = weight - rows_ref[x].astype(F32) * rate
    for slot in range(FRAG_HEADS):
        at = pl.ds(pl.multiple_of(order_ref[slot] * HEAD, HEAD), HEAD)
        incoming = global_ref[:, slot * HEAD : (slot + 1) * HEAD].astype(F32)
        new_ref[:, at] = 0.5 * new_ref[:, at] + 0.5 * incoming
    out_ref[0] = new_ref[...].astype(BF16)


def step(order, squares, rows, weight, new_global):
    return pl.pallas_call(
        step_kernel,
        grid=(4,),
        in_specs=[
            SMEM,
            pl.BlockSpec((8, 128), lambda i: (0, 0)),
            pl.BlockSpec((NX, 128, COLS), lambda i: (0, i, 0)),
            pl.BlockSpec((1, 128, KV), lambda i: (0, i, 0)),
            pl.BlockSpec((128, COLS), lambda i: (i, 0)),
        ],
        out_specs=pl.BlockSpec((1, 128, KV), lambda i: (0, i, 0)),
        out_shape=SDS((1, 512, KV), BF16),
        scratch_shapes=[pltpu.VMEM((128, KV), F32)],
        compiler_params=PARAMS,
        name="step",
    )(order, squares, rows, weight, new_global)


def call(kernel, outs, *args, scalars=0, flops=0):
    return pl.pallas_call(
        kernel,
        in_specs=[SMEM] * scalars + [pl.BlockSpec(memory_space=pltpu.VMEM)] * (len(args) - scalars),
        out_specs=jax.tree.map(lambda _: pl.BlockSpec(memory_space=pltpu.VMEM), outs),
        out_shape=outs,
        compiler_params=PARAMS,
        cost_estimate=pl.CostEstimate(flops=flops, bytes_accessed=4 << 20, transcendentals=0),
        name=kernel.__name__.removesuffix("_kernel"),
    )(*args)


def body(tokens, targets, local_weights, pending_delta, frag_order, global_frag, outer_momentum):
    place = lax.axis_index("fsdp")
    half = lax.rem(place, 2).astype(jnp.int32).reshape(1)
    my_x = lax.div(place, 2).astype(jnp.int32).reshape(1)
    dot_flops = 2 * 512 * 2048 * COLS

    with jax.named_scope("activations"):
        mine, other = split(half, tokens)
        arrived = flip(other, 1)
        near = gather(mine)

    with jax.named_scope("weight_columns"):
        blocks = call(pack_kernel, SDS((NX, 640, COLS), BF16), local_weights, targets)
        columns = exchange(blocks, "fsdp", X_GROUPS)

    with jax.named_scope("far_activations"):
        far = gather(arrived)

    with jax.named_scope("keys"):
        tall = (512, COLS)
        near_part, near_sent = call(
            near_kernel, (SDS(tall, F32), SDS(tall, BF16)), my_x, *near, columns, scalars=1, flops=dot_flops
        )
        far_rest = flip(near_sent, 1)
        near_turned = call(turn_kernel, SDS((2048, 512), BF16), *near)
        far_turned = call(turn_kernel, SDS((2048, 512), BF16), *far)
        far_sent, far_residual = call(
            far_kernel, (SDS(tall, BF16), SDS(tall, BF16)), *far, columns, far_rest, flops=dot_flops
        )
        near_rest = flip(far_sent, 1)

    with jax.named_scope("outer_sum"):
        by_z = lax.all_gather(pending_delta[0], "rep", axis_index_groups=Z_GROUPS)
        by_z = lax.optimization_barrier((by_z, near_sent[:16, :128]))[0]
        part = jnp.sum(by_z.astype(F32), axis=0).astype(BF16)
        by_l = lax.all_gather(part, "rep", axis_index_groups=L_GROUPS)
        mean = jnp.sum(by_l.astype(F32), axis=0) / lax.axis_size("rep")
        new_momentum = 0.9 * outer_momentum + mean
        new_global = (global_frag.astype(F32) - 0.7 * (mean + 0.9 * new_momentum)).astype(BF16)

    with jax.named_scope("gradient"):
        far_gradient = call(
            far_gradient_kernel, SDS((2048, COLS), F32), far_turned, far_residual, flops=dot_flops
        )
        gradient, squares = call(
            near_gradient_kernel,
            (SDS((NX, 512, COLS), BF16), SDS((8, 128), F32)),
            near_turned, near_part, near_rest, far_gradient, flops=dot_flops,
        )
        by_rows = exchange(gradient, "fsdp", X_GROUPS)
        squares = sum(gather(squares + flip(squares, 1)))

    with jax.named_scope("step"):
        new_weights = step(frag_order, squares, by_rows, local_weights, new_global)
    return (new_weights, new_global, new_momentum)


def solution(mesh):
    placed = (
        P(("rep", "fsdp"), None),
        P(("rep", "fsdp"), None),
        P("rep", "fsdp", None),
        P("rep", "fsdp", None),
        P(),
        P("fsdp", None),
        P("fsdp", None),
    )
    return jax.shard_map(
        body,
        mesh=mesh,
        in_specs=placed,
        out_specs=(P("rep", "fsdp", None), P("fsdp", None), P("fsdp", None)),
        check_vma=False,
    )
```

```python
import math

import jax
import jax.numpy as jnp
from jax import lax
from jax.experimental import pallas as pl
from jax.experimental.pallas import tpu as pltpu
from jax.sharding import PartitionSpec as P

D = 4096
HEAD = 128
FRAG_HEADS = 2
KV = 1024
NX = 4
COLS = KV // NX
FACTOR = 1.0 / math.sqrt(D)
F32 = jnp.float32
BF16 = jnp.bfloat16
SDS = jax.ShapeDtypeStruct
SMEM = pl.BlockSpec(memory_space=pltpu.SMEM)
PARAMS = pltpu.CompilerParams(vmem_limit_bytes=16 * 1024 * 1024)

X_GROUPS = [[x * 2 + h for x in range(NX)] for h in range(2)]
Z_GROUPS = [[z * 8 + l for z in range(8)] for l in range(8)]
Y_GROUPS = [[z * 8 + y * 2 + core for y in range(4)] for z in range(8) for core in range(2)]


def exchange(blocks, axis, groups):
    return lax.all_to_all(blocks, axis, 0, 0, axis_index_groups=groups, tiled=True)


def flip(block, mask):
    return lax.ppermute(block, "fsdp", [(i, i ^ mask) for i in range(8)])


def rotate(blocks):
    moves = [[(x * 2 + h, (x + d) % NX * 2 + h) for x in range(NX) for h in range(2)] for d in range(NX)]
    return [blocks[0]] + [lax.ppermute(blocks[d], "fsdp", moves[d]) for d in (1, 2, 3)]


def gather(block):
    return rotate([block] * NX)


def pack_kernel(place_ref, tokens_ref, weight_ref, targets_ref, other_ref, *message_refs):
    half, x = place_ref[0], place_ref[1]
    floated = tokens_ref[...].astype(F32)
    scale = lax.rsqrt(jnp.mean(floated * floated, axis=-1, keepdims=True) + 1e-06)
    for block in range(NX):
        lanes = slice(block * 512, (block + 1) * 512)
        for refs, side in ((message_refs, half), ((other_ref,), 1 - half)):
            start = pl.multiple_of((2 * block + side) * 512, 512)
            piece = (tokens_ref[:, pl.ds(start, 512)].astype(F32) * scale).astype(BF16)
            for ref in refs:
                ref[:128, lanes] = piece
    for d, ref in enumerate(message_refs):
        columns = pl.ds(pl.multiple_of(lax.rem(x + d, NX) * COLS, COLS), COLS)
        for j in range(8):
            lanes = slice(j * COLS, (j + 1) * COLS)
            ref[128:192, lanes] = weight_ref[0, j * 64 : (j + 1) * 64, columns]
            ref[192:, lanes] = targets_ref[j * 16 : (j + 1) * 16, columns]


def raw_keys(blocks, weight):
    lhs = jnp.concatenate([b[:128] for b in blocks], axis=0)
    return jnp.dot(lhs, weight, preferred_element_type=F32) * FACTOR


def near_kernel(place_ref, m0, m1, m2, m3, part_ref, sent_ref, weight_ref, turned_ref):
    messages = (m0, m1, m2, m3)
    for d, m in enumerate(messages):
        source = lax.rem(place_ref[1] - d + NX, NX)
        for j in range(8):
            rows = pl.ds(pl.multiple_of(source * 512 + j * 64, 64), 64)
            weight_ref[rows, :] = m[128:192, j * COLS : (j + 1) * COLS]
    keys = raw_keys(messages, weight_ref[...])
    for d, m in enumerate(messages):
        for j in range(8):
            rows = slice(d * 128 + j * 16, d * 128 + (j + 1) * 16)
            part = keys[rows] - m[192:, j * COLS : (j + 1) * COLS].astype(F32)
            part_ref[rows] = part
            sent_ref[rows] = part.astype(BF16)
        turned_ref[:, d * 128 : (d + 1) * 128] = m[:128].T


def far_kernel(*refs):
    sources, (sent_ref, residual_ref, delta_sum_ref), held, done = refs[:7], refs[7:10], refs[10:17], refs[17]
    fetches = [pltpu.make_async_copy(s, h, done.at[i]) for i, (s, h) in enumerate(zip(sources, held))]
    for fetch in fetches:
        fetch.start()
    for fetch in fetches[:6]:
        fetch.wait()
    keys = raw_keys(held[:4], held[4][...])
    sent_ref[...] = keys.astype(BF16)
    residual_ref[...] = (keys + held[5][...].astype(F32)).astype(BF16)
    fetches[6].wait()
    for rows in (slice(0, 256), slice(256, 512)):
        delta_sum_ref[rows] = jnp.sum(held[6][:, rows].astype(F32), axis=0).astype(BF16)


def turn_kernel(b0, b1, b2, b3, out_ref):
    for d, b in enumerate((b0, b1, b2, b3)):
        out_ref[:, d * 128 : (d + 1) * 128] = b[:128].T


def far_gradient_kernel(turned_ref, residual_ref, out_ref):
    out_ref[...] = jnp.dot(turned_ref[...], residual_ref[...], preferred_element_type=F32)


def near_gradient_kernel(turned_ref, part_ref, rest_ref, far_ref, out_ref, squares_ref):
    residual = (part_ref[...] + rest_ref[...].astype(F32)).astype(BF16)
    squares = jnp.zeros((8, COLS), F32)
    for x in range(NX):
        rows = slice(x * 512, (x + 1) * 512)
        near = jnp.dot(turned_ref[rows], residual, preferred_element_type=F32)
        gradient = (near + far_ref[rows]) * FACTOR
        out_ref[x, :512] = gradient.astype(BF16)
        out_ref[x, 512:] = jnp.zeros((16, COLS), BF16)
        squares += jnp.sum((gradient * gradient).reshape(64, 8, COLS), axis=0)
    squares_ref[...] = squares[:, :128] + squares[:, 128:]


def embed_kernel(squares_ref, _, out_ref):
    squares = squares_ref[...]
    high = squares.astype(BF16).astype(F32)
    middle = (squares - high).astype(BF16).astype(F32)
    low = squares - high - middle
    upper = jnp.concatenate([high, middle], axis=1)
    lower = jnp.concatenate([low, jnp.zeros((8, 128), F32)], axis=1)
    rows = jnp.concatenate([upper, lower], axis=0).astype(BF16)
    for x in range(NX):
        out_ref[x] = rows


def embed(squares, gradient):
    return pl.pallas_call(
        embed_kernel,
        grid=(1,),
        in_specs=[pl.BlockSpec((8, 128), lambda i: (0, 0)), pl.BlockSpec(memory_space=pl.ANY)],
        out_specs=pl.BlockSpec((NX, 16, COLS), lambda i: (0, 32, 0)),
        out_shape=SDS((NX, 528, COLS), BF16),
        input_output_aliases={1: 0},
        compiler_params=PARAMS,
        name="embed",
    )(squares, gradient)


def sum_kernel(blocks_ref, _, out_ref):
    out_ref[...] = jnp.sum(blocks_ref[...].astype(F32), axis=0)


def sum_blocks(blocks, later_than):
    return pl.pallas_call(
        sum_kernel,
        in_specs=[pl.BlockSpec(memory_space=pltpu.VMEM), pl.BlockSpec(memory_space=pl.ANY)],
        out_specs=pl.BlockSpec(memory_space=pltpu.VMEM),
        out_shape=SDS((512, 256), F32),
        compiler_params=PARAMS,
        name="sum_blocks",
    )(blocks, later_than)


def step_kernel(order_ref, squares_ref, rows_ref, weight_ref, global_ref, out_ref, new_ref):
    total = jnp.sum(squares_ref[...].astype(F32), axis=0)
    total = jnp.sum(total, axis=(0, 1), keepdims=True)
    rate = 0.25 * lax.rsqrt(total / (D * KV) + 1e-06)
    for x in range(NX):
        columns = slice(x * COLS, (x + 1) * COLS)
        weight = weight_ref[0, :, columns].astype(F32)
        new_ref[:, columns] = weight - rows_ref[x].astype(F32) * rate
    for slot in range(FRAG_HEADS):
        at = pl.ds(pl.multiple_of(order_ref[slot] * HEAD, HEAD), HEAD)
        incoming = global_ref[:, slot * HEAD : (slot + 1) * HEAD].astype(F32)
        new_ref[:, at] = 0.5 * new_ref[:, at] + 0.5 * incoming
    out_ref[0] = new_ref[...].astype(BF16)


def step(order, rows, weight, new_global):
    return pl.pallas_call(
        step_kernel,
        grid=(4,),
        in_specs=[
            SMEM,
            pl.BlockSpec((NX, 16, COLS), lambda i: (0, 32, 0)),
            pl.BlockSpec((NX, 128, COLS), lambda i: (0, i, 0)),
            pl.BlockSpec((1, 128, KV), lambda i: (0, i, 0)),
            pl.BlockSpec((128, COLS), lambda i: (i, 0)),
        ],
        out_specs=pl.BlockSpec((1, 128, KV), lambda i: (0, i, 0)),
        out_shape=SDS((1, 512, KV), BF16),
        scratch_shapes=[pltpu.VMEM((128, KV), F32)],
        compiler_params=PARAMS,
        name="step",
    )(order, rows, rows, weight, new_global)


def call(kernel, outs, *args, scalars=0, hbm=0, scratch=(), vmem_mib=16, flops=0):
    vmem = len(args) - scalars - hbm
    return pl.pallas_call(
        kernel,
        in_specs=[SMEM] * scalars
        + [pl.BlockSpec(memory_space=pltpu.VMEM)] * vmem
        + [pl.BlockSpec(memory_space=pltpu.HBM)] * hbm,
        scratch_shapes=scratch,
        out_specs=jax.tree.map(lambda _: pl.BlockSpec(memory_space=pltpu.VMEM), outs),
        out_shape=outs,
        compiler_params=pltpu.CompilerParams(vmem_limit_bytes=vmem_mib << 20),
        cost_estimate=pl.CostEstimate(flops=flops, bytes_accessed=4 << 20, transcendentals=0),
        name=kernel.__name__.removesuffix("_kernel"),
    )(*args)


def body(tokens, targets, local_weights, pending_delta, frag_order, global_frag, outer_momentum):
    index = lax.axis_index("fsdp")
    place = jnp.stack([lax.rem(index, 2), lax.div(index, 2)]).astype(jnp.int32)
    dot_flops = 2 * 512 * 2048 * COLS
    tall = (512, COLS)

    with jax.named_scope("activations"):
        other, *messages = call(
            pack_kernel,
            (SDS((128, 2048), BF16),) + (SDS((208, 2048), BF16),) * NX,
            place, tokens, local_weights, targets, scalars=1,
        )
        arrived = flip(other, 1)
        near = rotate(messages)
        far = gather(arrived)

    with jax.named_scope("near_keys"):
        near_part, near_sent, columns, near_turned = call(
            near_kernel,
            (SDS(tall, F32), SDS(tall, BF16), SDS((2048, COLS), BF16), SDS((2048, 512), BF16)),
            place, *near, scalars=1, flops=dot_flops,
        )
        far_rest = flip(near_sent, 1)

    with jax.named_scope("far_keys"):
        by_z = lax.all_gather(pending_delta[0], "rep", axis_index_groups=Z_GROUPS)
        far_sent, far_residual, delta_sum = call(
            far_kernel,
            (SDS(tall, BF16), SDS(tall, BF16), SDS((512, 256), BF16)),
            *far, columns, far_rest, by_z, flops=dot_flops, hbm=7, vmem_mib=58,
            scratch=[pltpu.VMEM((128, 2048), BF16)] * NX
            + [pltpu.VMEM((2048, COLS), BF16), pltpu.VMEM(tall, BF16), pltpu.VMEM((8, 512, 256), BF16)]
            + [pltpu.SemaphoreType.DMA((7,))],
        )
        by_y = lax.all_gather(delta_sum, "rep", axis_index_groups=Y_GROUPS)
        near_rest = flip(far_sent, 1)
        far_turned = call(turn_kernel, SDS((2048, 512), BF16), *far)

    with jax.named_scope("gradient"):
        far_gradient = call(
            far_gradient_kernel, SDS((2048, COLS), F32), far_turned, far_residual, flops=dot_flops
        )
        gradient, squares = call(
            near_gradient_kernel,
            (SDS((NX, 528, COLS), BF16), SDS((8, 128), F32)),
            near_turned, near_part, near_rest, far_gradient, flops=dot_flops,
        )
        squares = squares + flip(squares, 1)
        embedded = embed(squares, gradient)
        by_rows = exchange(embedded, "fsdp", X_GROUPS)

    with jax.named_scope("outer_sum"):
        core_sum = sum_blocks(by_y, embedded)
        total = core_sum + lax.ppermute(core_sum, "rep", [(i, i ^ 1) for i in range(64)])
        mean = total / lax.axis_size("rep")
        new_momentum = 0.9 * outer_momentum + mean
        new_global = (global_frag.astype(F32) - 0.7 * (mean + 0.9 * new_momentum)).astype(BF16)

    with jax.named_scope("step"):
        new_weights = step(frag_order, by_rows, local_weights, new_global)
    return (new_weights, new_global, new_momentum)


def solution(mesh):
    placed = (
        P(("rep", "fsdp"), None),
        P(("rep", "fsdp"), None),
        P("rep", "fsdp", None),
        P("rep", "fsdp", None),
        P(),
        P("fsdp", None),
        P("fsdp", None),
    )
    return jax.shard_map(
        body,
        mesh=mesh,
        in_specs=placed,
        out_specs=(P("rep", "fsdp", None), P("fsdp", None), P("fsdp", None)),
        check_vma=False,
    )
```

```python
import math

import jax
import jax.numpy as jnp
from jax import lax
from jax.experimental import pallas as pl
from jax.experimental.pallas import tpu as pltpu
from jax.sharding import PartitionSpec as P

D = 4096
HEAD = 128
FRAG_HEADS = 2
KV = 1024
NX = 4
COLS = KV // NX
FACTOR = 1.0 / math.sqrt(D)
F32 = jnp.float32
BF16 = jnp.bfloat16
SDS = jax.ShapeDtypeStruct
SMEM = pl.BlockSpec(memory_space=pltpu.SMEM)
PARAMS = pltpu.CompilerParams(vmem_limit_bytes=16 * 1024 * 1024)

X_GROUPS = [[x * 2 + h for x in range(NX)] for h in range(2)]
Z_GROUPS = [[z * 8 + l for z in range(8)] for l in range(8)]


def exchange(blocks, axis, groups):
    return lax.all_to_all(blocks, axis, 0, 0, axis_index_groups=groups, tiled=True)


def flip(block, mask):
    return lax.ppermute(block, "fsdp", [(i, i ^ mask) for i in range(8)])


def rotate(blocks):
    moves = [[(x * 2 + h, (x + d) % NX * 2 + h) for x in range(NX) for h in range(2)] for d in range(NX)]
    return [blocks[0]] + [lax.ppermute(blocks[d], "fsdp", moves[d]) for d in (1, 2, 3)]


def gather(block):
    return rotate([block] * NX)


def pack_kernel(place_ref, *refs):
    sources, other_ref, message_refs, held, done = refs[:3], refs[3], refs[4:8], refs[8:11], refs[11]
    fetches = [pltpu.make_async_copy(s, h, done.at[i]) for i, (s, h) in enumerate(zip(sources, held))]
    for fetch in fetches:
        fetch.start()
    half, x = place_ref[0], place_ref[1]
    tokens_ref, weight_ref, targets_ref = held
    fetches[0].wait()
    floated = tokens_ref[...].astype(F32)
    scale = lax.rsqrt(jnp.mean(floated * floated, axis=-1, keepdims=True) + 1e-06)
    for block in range(NX):
        lanes = slice(block * 512, (block + 1) * 512)
        for refs, side in ((message_refs, half), ((other_ref,), 1 - half)):
            start = pl.multiple_of((2 * block + side) * 512, 512)
            piece = (tokens_ref[:, pl.ds(start, 512)].astype(F32) * scale).astype(BF16)
            for ref in refs:
                ref[:128, lanes] = piece
    fetches[1].wait()
    fetches[2].wait()
    for d, ref in enumerate(message_refs):
        columns = pl.ds(pl.multiple_of(lax.rem(x + d, NX) * COLS, COLS), COLS)
        for j in range(8):
            lanes = slice(j * COLS, (j + 1) * COLS)
            ref[128:192, lanes] = weight_ref[0, j * 64 : (j + 1) * 64, columns]
            ref[192:, lanes] = targets_ref[j * 16 : (j + 1) * 16, columns]


def raw_keys(blocks, weight):
    lhs = jnp.concatenate([b[:128] for b in blocks], axis=0)
    return jnp.dot(lhs, weight, preferred_element_type=F32) * FACTOR


def near_kernel(place_ref, m0, m1, m2, m3, part_ref, sent_ref, weight_ref, turned_ref):
    messages = (m0, m1, m2, m3)
    for d, m in enumerate(messages):
        source = lax.rem(place_ref[1] - d + NX, NX)
        for j in range(8):
            rows = pl.ds(pl.multiple_of(source * 512 + j * 64, 64), 64)
            weight_ref[rows, :] = m[128:192, j * COLS : (j + 1) * COLS]
    keys = raw_keys(messages, weight_ref[...])
    for d, m in enumerate(messages):
        for j in range(8):
            rows = slice(d * 128 + j * 16, d * 128 + (j + 1) * 16)
            part = keys[rows] - m[192:, j * COLS : (j + 1) * COLS].astype(F32)
            part_ref[rows] = part
            sent_ref[rows] = part.astype(BF16)
        turned_ref[:, d * 128 : (d + 1) * 128] = m[:128].T


def far_kernel(b0, b1, b2, b3, weight_ref, rest_ref, sent_ref, residual_ref):
    keys = raw_keys((b0, b1, b2, b3), weight_ref[...])
    sent_ref[...] = keys.astype(BF16)
    residual_ref[...] = (keys + rest_ref[...].astype(F32)).astype(BF16)


def turn_kernel(b0, b1, b2, b3, out_ref):
    for d, b in enumerate((b0, b1, b2, b3)):
        out_ref[:, d * 128 : (d + 1) * 128] = b[:128].T


def far_gradient_kernel(turned_ref, residual_ref, out_ref):
    out_ref[...] = jnp.dot(turned_ref[...], residual_ref[...], preferred_element_type=F32)


def near_gradient_kernel(turned_ref, part_ref, rest_ref, far_ref, out_ref, squares_ref):
    residual = (part_ref[...] + rest_ref[...].astype(F32)).astype(BF16)
    squares = jnp.zeros((8, COLS), F32)
    for x in range(NX):
        rows = slice(x * 512, (x + 1) * 512)
        near = jnp.dot(turned_ref[rows], residual, preferred_element_type=F32)
        gradient = (near + far_ref[rows]) * FACTOR
        out_ref[x, :512] = gradient.astype(BF16)
        out_ref[x, 512:] = jnp.zeros((16, COLS), BF16)
        squares += jnp.sum((gradient * gradient).reshape(64, 8, COLS), axis=0)
    squares_ref[...] = squares[:, :128] + squares[:, 128:]


def embed_kernel(squares_ref, _, out_ref):
    squares = squares_ref[...]
    high = squares.astype(BF16).astype(F32)
    middle = (squares - high).astype(BF16).astype(F32)
    low = squares - high - middle
    upper = jnp.concatenate([high, middle], axis=1)
    lower = jnp.concatenate([low, jnp.zeros((8, 128), F32)], axis=1)
    rows = jnp.concatenate([upper, lower], axis=0).astype(BF16)
    for x in range(NX):
        out_ref[x] = rows


def embed(squares, gradient):
    return pl.pallas_call(
        embed_kernel,
        grid=(1,),
        in_specs=[pl.BlockSpec((8, 128), lambda i: (0, 0)), pl.BlockSpec(memory_space=pl.ANY)],
        out_specs=pl.BlockSpec((NX, 16, COLS), lambda i: (0, 32, 0)),
        out_shape=SDS((NX, 528, COLS), BF16),
        input_output_aliases={1: 0},
        compiler_params=PARAMS,
        name="embed",
    )(squares, gradient)


def step_kernel(order_ref, squares_ref, rows_ref, weight_ref, global_ref, out_ref, new_ref):
    total = jnp.sum(squares_ref[...].astype(F32), axis=0)
    total = jnp.sum(total, axis=(0, 1), keepdims=True)
    rate = 0.25 * lax.rsqrt(total / (D * KV) + 1e-06)
    for x in range(NX):
        columns = slice(x * COLS, (x + 1) * COLS)
        weight = weight_ref[0, :, columns].astype(F32)
        new_ref[:, columns] = weight - rows_ref[x].astype(F32) * rate
    for slot in range(FRAG_HEADS):
        at = pl.ds(pl.multiple_of(order_ref[slot] * HEAD, HEAD), HEAD)
        incoming = global_ref[:, slot * HEAD : (slot + 1) * HEAD].astype(F32)
        new_ref[:, at] = 0.5 * new_ref[:, at] + 0.5 * incoming
    out_ref[0] = new_ref[...].astype(BF16)


def step(order, rows, weight, new_global):
    return pl.pallas_call(
        step_kernel,
        grid=(4,),
        in_specs=[
            SMEM,
            pl.BlockSpec((NX, 16, COLS), lambda i: (0, 32, 0)),
            pl.BlockSpec((NX, 128, COLS), lambda i: (0, i, 0)),
            pl.BlockSpec((1, 128, KV), lambda i: (0, i, 0)),
            pl.BlockSpec((128, COLS), lambda i: (i, 0)),
        ],
        out_specs=pl.BlockSpec((1, 128, KV), lambda i: (0, i, 0)),
        out_shape=SDS((1, 512, KV), BF16),
        scratch_shapes=[pltpu.VMEM((128, KV), F32)],
        compiler_params=PARAMS,
        name="step",
    )(order, rows, rows, weight, new_global)


def call(kernel, outs, *args, scalars=0, hbm=0, scratch=(), vmem_mib=16, flops=0):
    vmem = len(args) - scalars - hbm
    return pl.pallas_call(
        kernel,
        in_specs=[SMEM] * scalars
        + [pl.BlockSpec(memory_space=pltpu.VMEM)] * vmem
        + [pl.BlockSpec(memory_space=pltpu.HBM)] * hbm,
        scratch_shapes=scratch,
        out_specs=jax.tree.map(lambda _: pl.BlockSpec(memory_space=pltpu.VMEM), outs),
        out_shape=outs,
        compiler_params=pltpu.CompilerParams(vmem_limit_bytes=vmem_mib << 20),
        cost_estimate=pl.CostEstimate(flops=flops, bytes_accessed=4 << 20, transcendentals=0),
        name=kernel.__name__.removesuffix("_kernel"),
    )(*args)


def body(tokens, targets, local_weights, pending_delta, frag_order, global_frag, outer_momentum):
    index = lax.axis_index("fsdp")
    place = jnp.stack([lax.rem(index, 2), lax.div(index, 2)]).astype(jnp.int32)
    dot_flops = 2 * 512 * 2048 * COLS
    tall = (512, COLS)

    with jax.named_scope("activations"):
        other, *messages = call(
            pack_kernel,
            (SDS((128, 2048), BF16),) + (SDS((208, 2048), BF16),) * NX,
            place, tokens, local_weights, targets, scalars=1, hbm=3, vmem_mib=58,
            scratch=[pltpu.VMEM(a.shape, BF16) for a in (tokens, local_weights, targets)]
            + [pltpu.SemaphoreType.DMA((3,))],
        )
        arrived = flip(other, 1)
        near = rotate(messages)
        far = gather(arrived)

    with jax.named_scope("near_keys"):
        near_part, near_sent, columns, near_turned = call(
            near_kernel,
            (SDS(tall, F32), SDS(tall, BF16), SDS((2048, COLS), BF16), SDS((2048, 512), BF16)),
            place, *near, scalars=1, flops=dot_flops,
        )
        far_rest = flip(near_sent, 1)

    with jax.named_scope("far_keys"):
        far_sent, far_residual = call(
            far_kernel, (SDS(tall, BF16), SDS(tall, BF16)), *far, columns, far_rest, flops=dot_flops
        )
        near_rest = flip(far_sent, 1)
        far_turned = call(turn_kernel, SDS((2048, 512), BF16), *far)

    with jax.named_scope("gradient"):
        far_gradient = call(
            far_gradient_kernel, SDS((2048, COLS), F32), far_turned, far_residual, flops=dot_flops
        )
        gradient, squares = call(
            near_gradient_kernel,
            (SDS((NX, 528, COLS), BF16), SDS((8, 128), F32)),
            near_turned, near_part, near_rest, far_gradient, flops=dot_flops,
        )
        squares = squares + flip(squares, 1)
        embedded = embed(squares, gradient)
        by_rows = exchange(embedded, "fsdp", X_GROUPS)

    with jax.named_scope("outer_sum"):
        by_z = exchange(pending_delta[0].reshape(8, 64, 256), "rep", Z_GROUPS)
        total = jnp.sum(by_z.astype(F32), axis=0)
        for mask in (1, 2, 4):
            total += lax.ppermute(total, "rep", [(i, i ^ mask) for i in range(64)])
        by_rows_z = exchange(jnp.broadcast_to(total[None], (8, 64, 256)), "rep", Z_GROUPS)
        mean = by_rows_z.reshape(512, 256) / lax.axis_size("rep")
        new_momentum = 0.9 * outer_momentum + mean
        new_global = (global_frag.astype(F32) - 0.7 * (mean + 0.9 * new_momentum)).astype(BF16)

    with jax.named_scope("step"):
        new_weights = step(frag_order, by_rows, local_weights, new_global)
    return (new_weights, new_global, new_momentum)


def solution(mesh):
    placed = (
        P(("rep", "fsdp"), None),
        P(("rep", "fsdp"), None),
        P("rep", "fsdp", None),
        P("rep", "fsdp", None),
        P(),
        P("fsdp", None),
        P("fsdp", None),
    )
    return jax.shard_map(
        body,
        mesh=mesh,
        in_specs=placed,
        out_specs=(P("rep", "fsdp", None), P("fsdp", None), P("fsdp", None)),
        check_vma=False,
    )
```

```python
import math

import jax
import jax.numpy as jnp
from jax import lax
from jax.experimental import pallas as pl
from jax.experimental.pallas import tpu as pltpu
from jax.sharding import PartitionSpec as P

D = 4096
HEAD = 128
FRAG_HEADS = 2
KV = 1024
NX = 4
COLS = KV // NX
FACTOR = 1.0 / math.sqrt(D)
F32 = jnp.float32
BF16 = jnp.bfloat16
SDS = jax.ShapeDtypeStruct
SMEM = pl.BlockSpec(memory_space=pltpu.SMEM)
PARAMS = pltpu.CompilerParams(vmem_limit_bytes=16 * 1024 * 1024)

X_GROUPS = [[x * 2 + h for x in range(NX)] for h in range(2)]
Z_GROUPS = [[z * 8 + l for z in range(8)] for l in range(8)]


def exchange(blocks, axis, groups):
    return lax.all_to_all(blocks, axis, 0, 0, axis_index_groups=groups, tiled=True)


def flip(block, mask):
    return lax.ppermute(block, "fsdp", [(i, i ^ mask) for i in range(8)])


def rotate(blocks):
    moves = [[(x * 2 + h, (x + d) % NX * 2 + h) for x in range(NX) for h in range(2)] for d in range(NX)]
    return [blocks[0]] + [lax.ppermute(blocks[d], "fsdp", moves[d]) for d in (1, 2, 3)]


def gather(block):
    return rotate([block] * NX)


def pack_kernel(place_ref, *refs):
    sources, other_ref, message_refs, held, done = refs[:3], refs[3], refs[4:8], refs[8:11], refs[11]
    fetches = [pltpu.make_async_copy(s, h, done.at[i]) for i, (s, h) in enumerate(zip(sources, held))]
    for fetch in fetches:
        fetch.start()
    half, x = place_ref[0], place_ref[1]
    tokens_ref, weight_ref, targets_ref = held
    fetches[0].wait()
    floated = tokens_ref[...].astype(F32)
    scale = lax.rsqrt(jnp.mean(floated * floated, axis=-1, keepdims=True) + 1e-06)
    for block in range(NX):
        lanes = slice(block * 512, (block + 1) * 512)
        for refs, side in ((message_refs, half), ((other_ref,), 1 - half)):
            start = pl.multiple_of((2 * block + side) * 512, 512)
            piece = (tokens_ref[:, pl.ds(start, 512)].astype(F32) * scale).astype(BF16)
            for ref in refs:
                ref[:128, lanes] = piece
    fetches[1].wait()
    fetches[2].wait()
    for d, ref in enumerate(message_refs):
        columns = pl.ds(pl.multiple_of(lax.rem(x + d, NX) * COLS, COLS), COLS)
        for j in range(8):
            lanes = slice(j * COLS, (j + 1) * COLS)
            ref[128:192, lanes] = weight_ref[0, j * 64 : (j + 1) * 64, columns]
            ref[192:, lanes] = targets_ref[j * 16 : (j + 1) * 16, columns]


def raw_keys(blocks, weight):
    lhs = jnp.concatenate([b[:128] for b in blocks], axis=0)
    return jnp.dot(lhs, weight, preferred_element_type=F32) * FACTOR


def near_kernel(place_ref, m0, m1, m2, m3, arrived_ref, part_ref, sent_ref, weight_ref, turned_ref, first_ref):
    messages = (m0, m1, m2, m3)
    for d, m in enumerate(messages):
        source = lax.rem(place_ref[1] - d + NX, NX)
        for j in range(8):
            rows = pl.ds(pl.multiple_of(source * 512 + j * 64, 64), 64)
            weight_ref[rows, :] = m[128:192, j * COLS : (j + 1) * COLS]
    keys = raw_keys((*messages, arrived_ref), weight_ref[...])
    first_ref[...] = keys[512:]
    sent_ref[512:] = keys[512:].astype(BF16)
    for d, m in enumerate(messages):
        for j in range(8):
            rows = slice(d * 128 + j * 16, d * 128 + (j + 1) * 16)
            part = keys[rows] - m[192:, j * COLS : (j + 1) * COLS].astype(F32)
            part_ref[rows] = part
            sent_ref[rows] = part.astype(BF16)
        turned_ref[:, d * 128 : (d + 1) * 128] = m[:128].T


def far_kernel(*refs):
    *blocks, weight_ref, keys_ref, sent_ref = refs
    keys_ref[...] = raw_keys(blocks, weight_ref[...])
    sent_ref[...] = keys_ref[...].astype(BF16)


def turn_kernel(b0, b1, b3, b2, out_ref):
    for i, b in enumerate((b0, b1, b3, b2)):
        out_ref[:, i * 128 : (i + 1) * 128] = b[...].T


def far_gradient_kernel(turned_ref, first_ref, sides_ref, last_ref, rest_ref, out_ref):
    keys = (first_ref[...], sides_ref[:128], sides_ref[128:], last_ref[...])
    rests = (rest_ref[:128], rest_ref[128:256], rest_ref[384:512], rest_ref[256:384])
    residual = jnp.concatenate([(k + r.astype(F32)).astype(BF16) for k, r in zip(keys, rests)], axis=0)
    out_ref[...] = jnp.dot(turned_ref[...], residual, preferred_element_type=F32)


def near_gradient_kernel(turned_ref, part_ref, rest_ref, sides_ref, last_ref, far_ref, out_ref, squares_ref):
    rests = (rest_ref[512:], sides_ref[:128], last_ref[...], sides_ref[128:])
    rest = jnp.concatenate([r.astype(F32) for r in rests], axis=0)
    residual = (part_ref[...] + rest).astype(BF16)
    squares = jnp.zeros((8, COLS), F32)
    for x in range(NX):
        rows = slice(x * 512, (x + 1) * 512)
        near = jnp.dot(turned_ref[rows], residual, preferred_element_type=F32)
        gradient = (near + far_ref[rows]) * FACTOR
        out_ref[x, :512] = gradient.astype(BF16)
        out_ref[x, 512:] = jnp.zeros((16, COLS), BF16)
        squares += jnp.sum((gradient * gradient).reshape(64, 8, COLS), axis=0)
    squares_ref[...] = squares[:, :128] + squares[:, 128:]


def embed_kernel(squares_ref, _, out_ref):
    squares = squares_ref[...]
    high = squares.astype(BF16).astype(F32)
    middle = (squares - high).astype(BF16).astype(F32)
    low = squares - high - middle
    upper = jnp.concatenate([high, middle], axis=1)
    lower = jnp.concatenate([low, jnp.zeros((8, 128), F32)], axis=1)
    rows = jnp.concatenate([upper, lower], axis=0).astype(BF16)
    for x in range(NX):
        out_ref[x] = rows


def embed(squares, gradient):
    return pl.pallas_call(
        embed_kernel,
        grid=(1,),
        in_specs=[pl.BlockSpec((8, 128), lambda i: (0, 0)), pl.BlockSpec(memory_space=pl.ANY)],
        out_specs=pl.BlockSpec((NX, 16, COLS), lambda i: (0, 32, 0)),
        out_shape=SDS((NX, 528, COLS), BF16),
        input_output_aliases={1: 0},
        compiler_params=PARAMS,
        name="embed",
    )(squares, gradient)


def sum_kernel(blocks_ref, _, out_ref):
    out_ref[...] = jnp.sum(blocks_ref[...].astype(F32), axis=0)


def step_kernel(order_ref, squares_ref, rows_ref, weight_ref, global_ref, out_ref, new_ref):
    total = jnp.sum(squares_ref[...].astype(F32), axis=0)
    total = jnp.sum(total, axis=(0, 1), keepdims=True)
    rate = 0.25 * lax.rsqrt(total / (D * KV) + 1e-06)
    for x in range(NX):
        columns = slice(x * COLS, (x + 1) * COLS)
        weight = weight_ref[0, :, columns].astype(F32)
        new_ref[:, columns] = weight - rows_ref[x].astype(F32) * rate
    for slot in range(FRAG_HEADS):
        at = pl.ds(pl.multiple_of(order_ref[slot] * HEAD, HEAD), HEAD)
        incoming = global_ref[:, slot * HEAD : (slot + 1) * HEAD].astype(F32)
        new_ref[:, at] = 0.5 * new_ref[:, at] + 0.5 * incoming
    out_ref[0] = new_ref[...].astype(BF16)


def step(order, rows, weight, new_global):
    return pl.pallas_call(
        step_kernel,
        grid=(4,),
        in_specs=[
            SMEM,
            pl.BlockSpec((NX, 16, COLS), lambda i: (0, 32, 0)),
            pl.BlockSpec((NX, 128, COLS), lambda i: (0, i, 0)),
            pl.BlockSpec((1, 128, KV), lambda i: (0, i, 0)),
            pl.BlockSpec((128, COLS), lambda i: (i, 0)),
        ],
        out_specs=pl.BlockSpec((1, 128, KV), lambda i: (0, i, 0)),
        out_shape=SDS((1, 512, KV), BF16),
        scratch_shapes=[pltpu.VMEM((128, KV), F32)],
        compiler_params=PARAMS,
        name="step",
    )(order, rows, rows, weight, new_global)


def call(kernel, outs, *args, scalars=0, hbm=0, scratch=(), vmem_mib=16, flops=0):
    vmem = len(args) - scalars - hbm
    return pl.pallas_call(
        kernel,
        in_specs=[SMEM] * scalars
        + [pl.BlockSpec(memory_space=pltpu.VMEM)] * vmem
        + [pl.BlockSpec(memory_space=pltpu.HBM)] * hbm,
        scratch_shapes=scratch,
        out_specs=jax.tree.map(lambda _: pl.BlockSpec(memory_space=pltpu.VMEM), outs),
        out_shape=outs,
        compiler_params=pltpu.CompilerParams(vmem_limit_bytes=vmem_mib << 20),
        cost_estimate=pl.CostEstimate(flops=flops, bytes_accessed=4 << 20, transcendentals=0),
        name=kernel.__name__.removesuffix("_kernel"),
    )(*args)


def body(tokens, targets, local_weights, pending_delta, frag_order, global_frag, outer_momentum):
    index = lax.axis_index("fsdp")
    place = jnp.stack([lax.rem(index, 2), lax.div(index, 2)]).astype(jnp.int32)
    dot_flops = 2 * 512 * 2048 * COLS
    tall = (512, COLS)

    with jax.named_scope("activations"):
        other, *messages = call(
            pack_kernel,
            (SDS((128, 2048), BF16),) + (SDS((208, 2048), BF16),) * NX,
            place, tokens, local_weights, targets, scalars=1, hbm=3, vmem_mib=58,
            scratch=[pltpu.VMEM(a.shape, BF16) for a in (tokens, local_weights, targets)]
            + [pltpu.SemaphoreType.DMA((3,))],
        )
        arrived = flip(other, 1)
        near = rotate(messages)
        far = gather(arrived)

    with jax.named_scope("near_keys"):
        near_part, near_sent, columns, near_turned, first_keys = call(
            near_kernel,
            (SDS(tall, F32), SDS((640, COLS), BF16), SDS((2048, COLS), BF16), SDS((2048, 512), BF16), SDS((128, COLS), F32)),
            place, *near, arrived, scalars=1, flops=dot_flops,
        )
        rest = flip(near_sent, 1)

    with jax.named_scope("far_keys"):
        sides_keys, sides_sent = call(
            far_kernel, (SDS((256, COLS), F32), SDS((256, COLS), BF16)), far[1], far[3], columns, flops=dot_flops // 2
        )
        sides_rest = flip(sides_sent, 1)
        last_keys, last_sent = call(
            far_kernel, (SDS((128, COLS), F32), SDS((128, COLS), BF16)), far[2], columns, flops=dot_flops // 4
        )
        last_rest = flip(last_sent, 1)
        far_turned = call(turn_kernel, SDS((2048, 512), BF16), far[0], far[1], far[3], far[2])

    with jax.named_scope("gradient"):
        far_gradient = call(
            far_gradient_kernel, SDS((2048, COLS), F32),
            far_turned, first_keys, sides_keys, last_keys, rest, flops=dot_flops,
        )
        gradient, squares = call(
            near_gradient_kernel,
            (SDS((NX, 528, COLS), BF16), SDS((8, 128), F32)),
            near_turned, near_part, rest, sides_rest, last_rest, far_gradient, flops=dot_flops,
        )
        squares = squares + flip(squares, 1)
        embedded = embed(squares, gradient)
        by_rows = exchange(embedded, "fsdp", X_GROUPS)

    with jax.named_scope("outer_sum"):
        by_z = exchange(pending_delta[0].reshape(8, 64, 256), "rep", Z_GROUPS)
        total = call(sum_kernel, SDS((64, 256), F32), by_z, arrived, hbm=1)
        for mask in (1, 2, 4):
            total += lax.ppermute(total, "rep", [(i, i ^ mask) for i in range(64)])
        by_rows_z = exchange(jnp.broadcast_to(total[None], (8, 64, 256)), "rep", Z_GROUPS)
        mean = by_rows_z.reshape(512, 256) / lax.axis_size("rep")
        new_momentum = 0.9 * outer_momentum + mean
        new_global = (global_frag.astype(F32) - 0.7 * (mean + 0.9 * new_momentum)).astype(BF16)

    with jax.named_scope("step"):
        new_weights = step(frag_order, by_rows, local_weights, new_global)
    return (new_weights, new_global, new_momentum)


def solution(mesh):
    placed = (
        P(("rep", "fsdp"), None),
        P(("rep", "fsdp"), None),
        P("rep", "fsdp", None),
        P("rep", "fsdp", None),
        P(),
        P("fsdp", None),
        P("fsdp", None),
    )
    return jax.shard_map(
        body,
        mesh=mesh,
        in_specs=placed,
        out_specs=(P("rep", "fsdp", None), P("fsdp", None), P("fsdp", None)),
        check_vma=False,
    )
```

```python
import math

import jax
import jax.numpy as jnp
from jax import lax
from jax.experimental import pallas as pl
from jax.experimental.pallas import tpu as pltpu
from jax.sharding import PartitionSpec as P

D = 4096
HEAD = 128
FRAG_HEADS = 2
KV = 1024
NX = 4
COLS = KV // NX
FACTOR = 1.0 / math.sqrt(D)
F32 = jnp.float32
BF16 = jnp.bfloat16
SDS = jax.ShapeDtypeStruct
SMEM = pl.BlockSpec(memory_space=pltpu.SMEM)
PARAMS = pltpu.CompilerParams(vmem_limit_bytes=16 * 1024 * 1024)

X_GROUPS = [[x * 2 + h for x in range(NX)] for h in range(2)]
Z_GROUPS = [[z * 8 + l for z in range(8)] for l in range(8)]


def exchange(blocks, axis, groups):
    return lax.all_to_all(blocks, axis, 0, 0, axis_index_groups=groups, tiled=True)


def flip(block, mask):
    return lax.ppermute(block, "fsdp", [(i, i ^ mask) for i in range(8)])


def rotate(blocks):
    moves = [[(x * 2 + h, (x + d) % NX * 2 + h) for x in range(NX) for h in range(2)] for d in range(NX)]
    return [blocks[0]] + [lax.ppermute(blocks[d], "fsdp", moves[d]) for d in (1, 2, 3)]


def gather(block):
    return rotate([block] * NX)


def pack_kernel(index_ref, *refs):
    sources, outs, held, (mine_ref, away_ref, columns_ref), (fetched, stored) = refs[:3], refs[3:8], refs[8:11], refs[11:14], refs[14:]
    fetches = [pltpu.make_async_copy(s, h, fetched.at[i]) for i, (s, h) in enumerate(zip(sources, held))]
    for fetch in fetches:
        fetch.start()
    half, x = lax.rem(index_ref[0], 2), lax.div(index_ref[0], 2)
    tokens_ref, weight_ref, targets_ref = held
    fetches[0].wait()
    floated = tokens_ref[...].astype(F32)
    scale = lax.rsqrt(jnp.mean(floated * floated, axis=-1, keepdims=True) + 1e-06)
    for ref, side in ((away_ref, 1 - half), (mine_ref, half)):
        for block in range(NX):
            start = pl.multiple_of((2 * block + side) * 512, 512)
            piece = tokens_ref[:, pl.ds(start, 512)].astype(F32) * scale
            ref[:, block * 512 : (block + 1) * 512] = piece.astype(BF16)
    stores = [pltpu.make_async_copy(away_ref, outs[0], stored.at[0])]
    stores += [pltpu.make_async_copy(mine_ref, out.at[:128], stored.at[1 + d]) for d, out in enumerate(outs[1:])]
    for store in stores:
        store.start()
    fetches[1].wait()
    fetches[2].wait()
    for d, out in enumerate(outs[1:]):
        columns = pl.ds(pl.multiple_of(lax.rem(x + d, NX) * COLS, COLS), COLS)
        for j in range(8):
            lanes = slice(j * COLS, (j + 1) * COLS)
            columns_ref[d, :64, lanes] = weight_ref[0, j * 64 : (j + 1) * 64, columns]
            columns_ref[d, 64:, lanes] = targets_ref[j * 16 : (j + 1) * 16, columns]
        store = pltpu.make_async_copy(columns_ref.at[d], out.at[128:], stored.at[5 + d])
        store.start()
        stores.append(store)
    for store in stores:
        store.wait()


def raw_keys(blocks, weight):
    lhs = jnp.concatenate([b[:128] for b in blocks], axis=0)
    return jnp.dot(lhs, weight, preferred_element_type=F32) * FACTOR


def near_kernel(index_ref, m0, m1, m2, m3, arrived_ref, part_ref, sent_ref, weight_ref, turned_ref, first_ref):
    messages = (m0, m1, m2, m3)
    for d, m in enumerate(messages):
        source = lax.rem(lax.div(index_ref[0], 2) - d + NX, NX)
        for j in range(8):
            rows = pl.ds(pl.multiple_of(source * 512 + j * 64, 64), 64)
            weight_ref[rows, :] = m[128:192, j * COLS : (j + 1) * COLS]
    keys = raw_keys((*messages, arrived_ref), weight_ref[...])
    first_ref[...] = keys[512:]
    sent_ref[512:] = keys[512:].astype(BF16)
    for d, m in enumerate(messages):
        for j in range(8):
            rows = slice(d * 128 + j * 16, d * 128 + (j + 1) * 16)
            part = keys[rows] - m[192:, j * COLS : (j + 1) * COLS].astype(F32)
            part_ref[rows] = part
            sent_ref[rows] = part.astype(BF16)
        turned_ref[:, d * 128 : (d + 1) * 128] = m[:128].T


def far_kernel(*refs):
    *blocks, weight_ref, keys_ref, sent_ref = refs
    keys_ref[...] = raw_keys(blocks, weight_ref[...])
    sent_ref[...] = keys_ref[...].astype(BF16)


def turn_kernel(b0, b1, b3, b2, out_ref):
    for i, b in enumerate((b0, b1, b3, b2)):
        out_ref[:, i * 128 : (i + 1) * 128] = b[...].T


def far_gradient_kernel(turned_ref, first_ref, sides_ref, last_ref, rest_ref, out_ref):
    keys = (first_ref[...], sides_ref[:128], sides_ref[128:], last_ref[...])
    rests = (rest_ref[:128], rest_ref[128:256], rest_ref[384:512], rest_ref[256:384])
    residual = jnp.concatenate([(k + r.astype(F32)).astype(BF16) for k, r in zip(keys, rests)], axis=0)
    out_ref[...] = jnp.dot(turned_ref[...], residual, preferred_element_type=F32)


def near_gradient_kernel(turned_ref, part_ref, rest_ref, sides_ref, last_ref, far_ref, out_ref, squares_ref):
    rests = (rest_ref[512:], sides_ref[:128], last_ref[...], sides_ref[128:])
    rest = jnp.concatenate([r.astype(F32) for r in rests], axis=0)
    residual = (part_ref[...] + rest).astype(BF16)
    squares = jnp.zeros((8, COLS), F32)
    for x in range(NX):
        rows = slice(x * 512, (x + 1) * 512)
        near = jnp.dot(turned_ref[rows], residual, preferred_element_type=F32)
        gradient = (near + far_ref[rows]) * FACTOR
        out_ref[x, :512] = gradient.astype(BF16)
        out_ref[x, 512:] = jnp.zeros((16, COLS), BF16)
        squares += jnp.sum((gradient * gradient).reshape(64, 8, COLS), axis=0)
    squares_ref[...] = squares[:, :128] + squares[:, 128:]


def embed_kernel(squares_ref, _, out_ref):
    squares = squares_ref[...]
    high = squares.astype(BF16).astype(F32)
    middle = (squares - high).astype(BF16).astype(F32)
    low = squares - high - middle
    upper = jnp.concatenate([high, middle], axis=1)
    lower = jnp.concatenate([low, jnp.zeros((8, 128), F32)], axis=1)
    rows = jnp.concatenate([upper, lower], axis=0).astype(BF16)
    for x in range(NX):
        out_ref[x] = rows


def embed(squares, gradient):
    return pl.pallas_call(
        embed_kernel,
        grid=(1,),
        in_specs=[pl.BlockSpec((8, 128), lambda i: (0, 0)), pl.BlockSpec(memory_space=pl.ANY)],
        out_specs=pl.BlockSpec((NX, 16, COLS), lambda i: (0, 32, 0)),
        out_shape=SDS((NX, 528, COLS), BF16),
        input_output_aliases={1: 0},
        compiler_params=PARAMS,
        name="embed",
    )(squares, gradient)


def sum_kernel(blocks_ref, _, out_ref):
    out_ref[...] = jnp.sum(blocks_ref[...].astype(F32), axis=0)


def step_kernel(order_ref, squares_ref, rows_ref, weight_ref, global_ref, out_ref, new_ref):
    total = jnp.sum(squares_ref[...].astype(F32), axis=0)
    total = jnp.sum(total, axis=(0, 1), keepdims=True)
    rate = 0.25 * lax.rsqrt(total / (D * KV) + 1e-06)
    for x in range(NX):
        columns = slice(x * COLS, (x + 1) * COLS)
        weight = weight_ref[0, :, columns].astype(F32)
        new_ref[:, columns] = weight - rows_ref[x].astype(F32) * rate
    for slot in range(FRAG_HEADS):
        at = pl.ds(pl.multiple_of(order_ref[slot] * HEAD, HEAD), HEAD)
        incoming = global_ref[:, slot * HEAD : (slot + 1) * HEAD].astype(F32)
        new_ref[:, at] = 0.5 * new_ref[:, at] + 0.5 * incoming
    out_ref[0] = new_ref[...].astype(BF16)


def step(order, rows, weight, new_global):
    return pl.pallas_call(
        step_kernel,
        grid=(4,),
        in_specs=[
            SMEM,
            pl.BlockSpec((NX, 16, COLS), lambda i: (0, 32, 0)),
            pl.BlockSpec((NX, 128, COLS), lambda i: (0, i, 0)),
            pl.BlockSpec((1, 128, KV), lambda i: (0, i, 0)),
            pl.BlockSpec((128, COLS), lambda i: (i, 0)),
        ],
        out_specs=pl.BlockSpec((1, 128, KV), lambda i: (0, i, 0)),
        out_shape=SDS((1, 512, KV), BF16),
        scratch_shapes=[pltpu.VMEM((128, KV), F32)],
        compiler_params=PARAMS,
        name="step",
    )(order, rows, rows, weight, new_global)


def call(kernel, outs, *args, scalars=0, hbm=0, scratch=(), vmem_mib=16, out_space=pltpu.VMEM, flops=0):
    vmem = len(args) - scalars - hbm
    return pl.pallas_call(
        kernel,
        in_specs=[SMEM] * scalars
        + [pl.BlockSpec(memory_space=pltpu.VMEM)] * vmem
        + [pl.BlockSpec(memory_space=pltpu.HBM)] * hbm,
        scratch_shapes=scratch,
        out_specs=jax.tree.map(lambda _: pl.BlockSpec(memory_space=out_space), outs),
        out_shape=outs,
        compiler_params=pltpu.CompilerParams(vmem_limit_bytes=vmem_mib << 20),
        cost_estimate=pl.CostEstimate(flops=flops, bytes_accessed=4 << 20, transcendentals=0),
        name=kernel.__name__.removesuffix("_kernel"),
    )(*args)


def body(tokens, targets, local_weights, pending_delta, frag_order, global_frag, outer_momentum):
    index = lax.axis_index("fsdp").astype(jnp.int32).reshape(1)
    dot_flops = 2 * 512 * 2048 * COLS
    tall = (512, COLS)

    with jax.named_scope("activations"):
        other, *messages = call(
            pack_kernel,
            (SDS((128, 2048), BF16),) + (SDS((208, 2048), BF16),) * NX,
            index, tokens, local_weights, targets, scalars=1, hbm=3, out_space=pltpu.HBM, vmem_mib=58,
            scratch=[pltpu.VMEM(a.shape, BF16) for a in (tokens, local_weights, targets)]
            + [pltpu.VMEM((128, 2048), BF16)] * 2
            + [pltpu.VMEM((NX, 80, 2048), BF16), pltpu.SemaphoreType.DMA((3,)), pltpu.SemaphoreType.DMA((9,))],
        )
        arrived = flip(other, 1)
        near = rotate(messages)
        far = gather(arrived)

    with jax.named_scope("near_keys"):
        near_part, near_sent, columns, near_turned, first_keys = call(
            near_kernel,
            (SDS(tall, F32), SDS((640, COLS), BF16), SDS((2048, COLS), BF16), SDS((2048, 512), BF16), SDS((128, COLS), F32)),
            index, *near, arrived, scalars=1, flops=dot_flops,
        )
        rest = flip(near_sent, 1)

    with jax.named_scope("far_keys"):
        sides_keys, sides_sent = call(
            far_kernel, (SDS((256, COLS), F32), SDS((256, COLS), BF16)), far[1], far[3], columns, flops=dot_flops // 2
        )
        sides_rest = flip(sides_sent, 1)
        last_keys, last_sent = call(
            far_kernel, (SDS((128, COLS), F32), SDS((128, COLS), BF16)), far[2], columns, flops=dot_flops // 4
        )
        last_rest = flip(last_sent, 1)
        far_turned = call(turn_kernel, SDS((2048, 512), BF16), far[0], far[1], far[3], far[2])

    with jax.named_scope("gradient"):
        far_gradient = call(
            far_gradient_kernel, SDS((2048, COLS), F32),
            far_turned, first_keys, sides_keys, last_keys, rest, flops=dot_flops,
        )
        gradient, squares = call(
            near_gradient_kernel,
            (SDS((NX, 528, COLS), BF16), SDS((8, 128), F32)),
            near_turned, near_part, rest, sides_rest, last_rest, far_gradient, flops=dot_flops,
        )
        squares = squares + flip(squares, 1)
        embedded = embed(squares, gradient)
        by_rows = exchange(embedded, "fsdp", X_GROUPS)

    with jax.named_scope("outer_sum"):
        by_z = exchange(pending_delta[0].reshape(8, 64, 256), "rep", Z_GROUPS)
        total = call(sum_kernel, SDS((64, 256), F32), by_z, arrived, hbm=1)
        for mask in (1, 2, 4):
            total += lax.ppermute(total, "rep", [(i, i ^ mask) for i in range(64)])
        by_rows_z = exchange(jnp.broadcast_to(total.astype(BF16)[None], (8, 64, 256)), "rep", Z_GROUPS)
        mean = by_rows_z.astype(F32).reshape(512, 256) / lax.axis_size("rep")
        new_momentum = 0.9 * outer_momentum + mean
        new_global = (global_frag.astype(F32) - 0.7 * (mean + 0.9 * new_momentum)).astype(BF16)

    with jax.named_scope("step"):
        new_weights = step(frag_order, by_rows, local_weights, new_global)
    return (new_weights, new_global, new_momentum)


def solution(mesh):
    placed = (
        P(("rep", "fsdp"), None),
        P(("rep", "fsdp"), None),
        P("rep", "fsdp", None),
        P("rep", "fsdp", None),
        P(),
        P("fsdp", None),
        P("fsdp", None),
    )
    return jax.shard_map(
        body,
        mesh=mesh,
        in_specs=placed,
        out_specs=(P("rep", "fsdp", None), P("fsdp", None), P("fsdp", None)),
        check_vma=False,
    )
```

```python
import math

import jax
import jax.numpy as jnp
from jax import lax
from jax.experimental import pallas as pl
from jax.experimental.pallas import tpu as pltpu
from jax.sharding import PartitionSpec as P

D = 4096
HEAD = 128
FRAG_HEADS = 2
KV = 1024
NX = 4
COLS = KV // NX
FACTOR = 1.0 / math.sqrt(D)
F32 = jnp.float32
BF16 = jnp.bfloat16
SDS = jax.ShapeDtypeStruct
SMEM = pl.BlockSpec(memory_space=pltpu.SMEM)
PARAMS = pltpu.CompilerParams(vmem_limit_bytes=16 * 1024 * 1024)

X_GROUPS = [[x * 2 + h for x in range(NX)] for h in range(2)]
L_GROUPS = [[z * 8 + l for l in range(8)] for z in range(8)]
Z_GROUPS = [[z * 8 + l for z in range(8)] for l in range(8)]


def exchange(blocks, axis, groups):
    return lax.all_to_all(blocks, axis, 0, 0, axis_index_groups=groups, tiled=True)


def flip(block, mask):
    return lax.ppermute(block, "fsdp", [(i, i ^ mask) for i in range(8)])


def rotate(blocks):
    moves = [[(x * 2 + h, (x + d) % NX * 2 + h) for x in range(NX) for h in range(2)] for d in range(NX)]
    return [blocks[0]] + [lax.ppermute(blocks[d], "fsdp", moves[d]) for d in (1, 2, 3)]


def gather(block):
    return rotate([block] * NX)


def pack_kernel(index_ref, *refs):
    sources, outs, held, (mine_ref, away_ref, columns_ref), (fetched, stored) = refs[:3], refs[3:8], refs[8:11], refs[11:14], refs[14:]
    fetches = [pltpu.make_async_copy(s, h, fetched.at[i]) for i, (s, h) in enumerate(zip(sources, held))]
    for fetch in fetches:
        fetch.start()
    half, x = lax.rem(index_ref[0], 2), lax.div(index_ref[0], 2)
    tokens_ref, weight_ref, targets_ref = held
    fetches[0].wait()
    floated = tokens_ref[...].astype(F32)
    scale = lax.rsqrt(jnp.mean(floated * floated, axis=-1, keepdims=True) + 1e-06)
    for ref, side in ((away_ref, 1 - half), (mine_ref, half)):
        for block in range(NX):
            start = pl.multiple_of((2 * block + side) * 512, 512)
            piece = tokens_ref[:, pl.ds(start, 512)].astype(F32) * scale
            ref[:, block * 512 : (block + 1) * 512] = piece.astype(BF16)
    stores = [pltpu.make_async_copy(away_ref, outs[0], stored.at[0])]
    stores += [pltpu.make_async_copy(mine_ref, out.at[:128], stored.at[1 + d]) for d, out in enumerate(outs[1:])]
    for store in stores:
        store.start()
    fetches[1].wait()
    fetches[2].wait()
    for d, out in enumerate(outs[1:]):
        columns = pl.ds(pl.multiple_of(lax.rem(x + d, NX) * COLS, COLS), COLS)
        for j in range(8):
            lanes = slice(j * COLS, (j + 1) * COLS)
            columns_ref[d, :64, lanes] = weight_ref[0, j * 64 : (j + 1) * 64, columns]
            columns_ref[d, 64:, lanes] = targets_ref[j * 16 : (j + 1) * 16, columns]
        store = pltpu.make_async_copy(columns_ref.at[d], out.at[128:], stored.at[5 + d])
        store.start()
        stores.append(store)
    for store in stores:
        store.wait()


def raw_keys(blocks, weight):
    lhs = jnp.concatenate([b[:128] for b in blocks], axis=0)
    return jnp.dot(lhs, weight, preferred_element_type=F32) * FACTOR


def near_kernel(index_ref, m0, m1, m2, m3, arrived_ref, part_ref, sent_ref, weight_ref, turned_ref, first_ref):
    messages = (m0, m1, m2, m3)
    for d, m in enumerate(messages):
        source = lax.rem(lax.div(index_ref[0], 2) - d + NX, NX)
        for j in range(8):
            rows = pl.ds(pl.multiple_of(source * 512 + j * 64, 64), 64)
            weight_ref[rows, :] = m[128:192, j * COLS : (j + 1) * COLS]
    keys = raw_keys((*messages, arrived_ref), weight_ref[...])
    first_ref[...] = keys[512:]
    sent_ref[512:] = keys[512:].astype(BF16)
    for d, m in enumerate(messages):
        for j in range(8):
            rows = slice(d * 128 + j * 16, d * 128 + (j + 1) * 16)
            part = keys[rows] - m[192:, j * COLS : (j + 1) * COLS].astype(F32)
            part_ref[rows] = part
            sent_ref[rows] = part.astype(BF16)
        turned_ref[:, d * 128 : (d + 1) * 128] = m[:128].T


def far_kernel(*refs):
    *blocks, weight_ref, _, keys_ref, sent_ref = refs
    keys_ref[...] = raw_keys(blocks, weight_ref[...])
    sent_ref[...] = keys_ref[...].astype(BF16)


def turn_kernel(b0, b1, b3, b2, out_ref):
    for i, b in enumerate((b0, b1, b3, b2)):
        out_ref[:, i * 128 : (i + 1) * 128] = b[...].T


def far_gradient_kernel(turned_ref, first_ref, sides_ref, last_ref, rest_ref, out_ref):
    keys = (first_ref[...], sides_ref[:128], sides_ref[128:], last_ref[...])
    rests = (rest_ref[:128], rest_ref[128:256], rest_ref[384:512], rest_ref[256:384])
    residual = jnp.concatenate([(k + r.astype(F32)).astype(BF16) for k, r in zip(keys, rests)], axis=0)
    out_ref[...] = jnp.dot(turned_ref[...], residual, preferred_element_type=F32)


def near_gradient_kernel(turned_ref, part_ref, rest_ref, sides_ref, last_ref, far_ref, out_ref, squares_ref):
    rests = (rest_ref[512:], sides_ref[:128], last_ref[...], sides_ref[128:])
    rest = jnp.concatenate([r.astype(F32) for r in rests], axis=0)
    residual = (part_ref[...] + rest).astype(BF16)
    squares = jnp.zeros((8, COLS), F32)
    for x in range(NX):
        rows = slice(x * 512, (x + 1) * 512)
        near = jnp.dot(turned_ref[rows], residual, preferred_element_type=F32)
        gradient = (near + far_ref[rows]) * FACTOR
        out_ref[x, :512] = gradient.astype(BF16)
        out_ref[x, 512:] = jnp.zeros((16, COLS), BF16)
        squares += jnp.sum((gradient * gradient).reshape(64, 8, COLS), axis=0)
    squares_ref[...] = squares[:, :128] + squares[:, 128:]


def embed_kernel(squares_ref, _, out_ref):
    squares = squares_ref[...]
    high = squares.astype(BF16).astype(F32)
    middle = (squares - high).astype(BF16).astype(F32)
    low = squares - high - middle
    upper = jnp.concatenate([high, middle], axis=1)
    lower = jnp.concatenate([low, jnp.zeros((8, 128), F32)], axis=1)
    rows = jnp.concatenate([upper, lower], axis=0).astype(BF16)
    for x in range(NX):
        out_ref[x] = rows


def embed(squares, gradient):
    return pl.pallas_call(
        embed_kernel,
        grid=(1,),
        in_specs=[pl.BlockSpec((8, 128), lambda i: (0, 0)), pl.BlockSpec(memory_space=pl.ANY)],
        out_specs=pl.BlockSpec((NX, 16, COLS), lambda i: (0, 32, 0)),
        out_shape=SDS((NX, 528, COLS), BF16),
        input_output_aliases={1: 0},
        compiler_params=PARAMS,
        name="embed",
    )(squares, gradient)


def sum_kernel(blocks_ref, *refs):
    total = jnp.sum(blocks_ref[...].astype(F32), axis=0).astype(refs[-1].dtype)
    for i in range(8):
        refs[-1][i] = total


def step_kernel(order_ref, squares_ref, rows_ref, weight_ref, global_ref, out_ref, new_ref):
    total = jnp.sum(squares_ref[...].astype(F32), axis=0)
    total = jnp.sum(total, axis=(0, 1), keepdims=True)
    rate = 0.25 * lax.rsqrt(total / (D * KV) + 1e-06)
    for x in range(NX):
        columns = slice(x * COLS, (x + 1) * COLS)
        weight = weight_ref[0, :, columns].astype(F32)
        new_ref[:, columns] = weight - rows_ref[x].astype(F32) * rate
    for slot in range(FRAG_HEADS):
        at = pl.ds(pl.multiple_of(order_ref[slot] * HEAD, HEAD), HEAD)
        incoming = global_ref[:, slot * HEAD : (slot + 1) * HEAD].astype(F32)
        new_ref[:, at] = 0.5 * new_ref[:, at] + 0.5 * incoming
    out_ref[0] = new_ref[...].astype(BF16)


def step(order, rows, weight, new_global):
    return pl.pallas_call(
        step_kernel,
        grid=(4,),
        in_specs=[
            SMEM,
            pl.BlockSpec((NX, 16, COLS), lambda i: (0, 32, 0)),
            pl.BlockSpec((NX, 128, COLS), lambda i: (0, i, 0)),
            pl.BlockSpec((1, 128, KV), lambda i: (0, i, 0)),
            pl.BlockSpec((128, COLS), lambda i: (i, 0)),
        ],
        out_specs=pl.BlockSpec((1, 128, KV), lambda i: (0, i, 0)),
        out_shape=SDS((1, 512, KV), BF16),
        scratch_shapes=[pltpu.VMEM((128, KV), F32)],
        compiler_params=PARAMS,
        name="step",
    )(order, rows, rows, weight, new_global)


def call(kernel, outs, *args, scalars=0, hbm=0, scratch=(), vmem_mib=16, out_space=pltpu.VMEM, flops=0):
    vmem = len(args) - scalars - hbm
    return pl.pallas_call(
        kernel,
        in_specs=[SMEM] * scalars
        + [pl.BlockSpec(memory_space=pltpu.VMEM)] * vmem
        + [pl.BlockSpec(memory_space=pltpu.HBM)] * hbm,
        scratch_shapes=scratch,
        out_specs=jax.tree.map(lambda _: pl.BlockSpec(memory_space=out_space), outs),
        out_shape=outs,
        compiler_params=pltpu.CompilerParams(vmem_limit_bytes=vmem_mib << 20),
        cost_estimate=pl.CostEstimate(flops=flops, bytes_accessed=4 << 20, transcendentals=0),
        name=kernel.__name__.removesuffix("_kernel"),
    )(*args)


def body(tokens, targets, local_weights, pending_delta, frag_order, global_frag, outer_momentum):
    index = lax.axis_index("fsdp").astype(jnp.int32).reshape(1)
    dot_flops = 2 * 512 * 2048 * COLS
    tall = (512, COLS)

    with jax.named_scope("activations"):
        other, *messages = call(
            pack_kernel,
            (SDS((128, 2048), BF16),) + (SDS((208, 2048), BF16),) * NX,
            index, tokens, local_weights, targets, scalars=1, hbm=3, out_space=pltpu.HBM, vmem_mib=58,
            scratch=[pltpu.VMEM(a.shape, BF16) for a in (tokens, local_weights, targets)]
            + [pltpu.VMEM((128, 2048), BF16)] * 2
            + [pltpu.VMEM((NX, 80, 2048), BF16), pltpu.SemaphoreType.DMA((3,)), pltpu.SemaphoreType.DMA((9,))],
        )
        arrived = flip(other, 1)
        near = rotate(messages)
        far = gather(arrived)

    with jax.named_scope("near_keys"):
        near_part, near_sent, columns, near_turned, first_keys = call(
            near_kernel,
            (SDS(tall, F32), SDS((640, COLS), BF16), SDS((2048, COLS), BF16), SDS((2048, 512), BF16), SDS((128, COLS), F32)),
            index, *near, arrived, scalars=1, flops=dot_flops,
        )
        rest = flip(near_sent, 1)

    with jax.named_scope("far_keys"):
        sides_keys, sides_sent = call(
            far_kernel, (SDS((256, COLS), F32), SDS((256, COLS), BF16)), far[1], far[3], columns, rest, flops=dot_flops // 2, hbm=1
        )
        sides_rest = flip(sides_sent, 1)
        last_keys, last_sent = call(
            far_kernel, (SDS((128, COLS), F32), SDS((128, COLS), BF16)), far[2], columns, rest, flops=dot_flops // 4, hbm=1
        )
        last_rest = flip(last_sent, 1)
        far_turned = call(turn_kernel, SDS((2048, 512), BF16), far[0], far[1], far[3], far[2])

    with jax.named_scope("gradient"):
        far_gradient = call(
            far_gradient_kernel, SDS((2048, COLS), F32),
            far_turned, first_keys, sides_keys, last_keys, rest, flops=dot_flops,
        )
        gradient, squares = call(
            near_gradient_kernel,
            (SDS((NX, 528, COLS), BF16), SDS((8, 128), F32)),
            near_turned, near_part, rest, sides_rest, last_rest, far_gradient, flops=dot_flops,
        )
        squares = squares + flip(squares, 1)
        embedded = embed(squares, gradient)
        by_rows = exchange(embedded, "fsdp", X_GROUPS)

    with jax.named_scope("outer_sum"):
        by_l = exchange(pending_delta[0].reshape(8, 64, 256), "rep", L_GROUPS)
        by_z = exchange(call(sum_kernel, SDS((8, 64, 256), BF16), by_l, arrived, hbm=1), "rep", Z_GROUPS)
        rows = exchange(call(sum_kernel, SDS((8, 64, 256), BF16), by_z), "rep", L_GROUPS)
        mean = rows.reshape(512, 256).astype(F32) / lax.axis_size("rep")
        new_momentum = 0.9 * outer_momentum + mean
        new_global = (global_frag.astype(F32) - 0.7 * (mean + 0.9 * new_momentum)).astype(BF16)

    with jax.named_scope("step"):
        new_weights = step(frag_order, by_rows, local_weights, new_global)
    return (new_weights, new_global, new_momentum)


def solution(mesh):
    placed = (
        P(("rep", "fsdp"), None),
        P(("rep", "fsdp"), None),
        P("rep", "fsdp", None),
        P("rep", "fsdp", None),
        P(),
        P("fsdp", None),
        P("fsdp", None),
    )
    return jax.shard_map(
        body,
        mesh=mesh,
        in_specs=placed,
        out_specs=(P("rep", "fsdp", None), P("fsdp", None), P("fsdp", None)),
        check_vma=False,
    )
```

```python
import math

import jax
import jax.numpy as jnp
from jax import lax
from jax.experimental import pallas as pl
from jax.experimental.pallas import tpu as pltpu
from jax.sharding import PartitionSpec as P

D = 4096
HEAD = 128
FRAG_HEADS = 2
KV = 1024
NX = 4
COLS = KV // NX
FACTOR = 1.0 / math.sqrt(D)
F32 = jnp.float32
BF16 = jnp.bfloat16
SDS = jax.ShapeDtypeStruct
SMEM = pl.BlockSpec(memory_space=pltpu.SMEM)
PARAMS = pltpu.CompilerParams(vmem_limit_bytes=16 * 1024 * 1024)

X_GROUPS = [[x * 2 + h for x in range(NX)] for h in range(2)]


def exchange(blocks, axis, groups):
    return lax.all_to_all(blocks, axis, 0, 0, axis_index_groups=groups, tiled=True)


def flip(block, mask):
    return lax.ppermute(block, "fsdp", [(i, i ^ mask) for i in range(8)])


def rotate(blocks):
    moves = [[(x * 2 + h, (x + d) % NX * 2 + h) for x in range(NX) for h in range(2)] for d in range(NX)]
    return [blocks[0]] + [lax.ppermute(blocks[d], "fsdp", moves[d]) for d in (1, 2, 3)]


def gather(block):
    return rotate([block] * NX)


def pack_kernel(index_ref, *refs):
    sources, outs, held, (mine_ref, away_ref, columns_ref), (fetched, stored) = refs[:3], refs[3:8], refs[8:11], refs[11:14], refs[14:]
    fetches = [pltpu.make_async_copy(s, h, fetched.at[i]) for i, (s, h) in enumerate(zip(sources, held))]
    for fetch in fetches:
        fetch.start()
    half, x = lax.rem(index_ref[0], 2), lax.div(index_ref[0], 2)
    tokens_ref, weight_ref, targets_ref = held
    fetches[0].wait()
    floated = tokens_ref[...].astype(F32)
    scale = lax.rsqrt(jnp.mean(floated * floated, axis=-1, keepdims=True) + 1e-06)
    for ref, side in ((away_ref, 1 - half), (mine_ref, half)):
        for block in range(NX):
            start = pl.multiple_of((2 * block + side) * 512, 512)
            piece = tokens_ref[:, pl.ds(start, 512)].astype(F32) * scale
            ref[:, block * 512 : (block + 1) * 512] = piece.astype(BF16)
    stores = [pltpu.make_async_copy(away_ref, outs[0], stored.at[0])]
    stores += [pltpu.make_async_copy(mine_ref, out.at[:128], stored.at[1 + d]) for d, out in enumerate(outs[1:])]
    for store in stores:
        store.start()
    fetches[1].wait()
    fetches[2].wait()
    for d, out in enumerate(outs[1:]):
        columns = pl.ds(pl.multiple_of(lax.rem(x + d, NX) * COLS, COLS), COLS)
        for j in range(8):
            lanes = slice(j * COLS, (j + 1) * COLS)
            columns_ref[d, :64, lanes] = weight_ref[0, j * 64 : (j + 1) * 64, columns]
            columns_ref[d, 64:, lanes] = targets_ref[j * 16 : (j + 1) * 16, columns]
        store = pltpu.make_async_copy(columns_ref.at[d], out.at[128:], stored.at[5 + d])
        store.start()
        stores.append(store)
    for store in stores:
        store.wait()


def raw_keys(blocks, weight):
    lhs = jnp.concatenate([b[:128] for b in blocks], axis=0)
    return jnp.dot(lhs, weight, preferred_element_type=F32) * FACTOR


def near_kernel(index_ref, m0, m1, m2, m3, arrived_ref, part_ref, sent_ref, weight_ref, turned_ref, first_ref):
    messages = (m0, m1, m2, m3)
    for d, m in enumerate(messages):
        source = lax.rem(lax.div(index_ref[0], 2) - d + NX, NX)
        for j in range(8):
            rows = pl.ds(pl.multiple_of(source * 512 + j * 64, 64), 64)
            weight_ref[rows, :] = m[128:192, j * COLS : (j + 1) * COLS]
    keys = raw_keys((*messages, arrived_ref), weight_ref[...])
    first_ref[...] = keys[512:]
    sent_ref[512:] = keys[512:].astype(BF16)
    for d, m in enumerate(messages):
        for j in range(8):
            rows = slice(d * 128 + j * 16, d * 128 + (j + 1) * 16)
            part = keys[rows] - m[192:, j * COLS : (j + 1) * COLS].astype(F32)
            part_ref[rows] = part
            sent_ref[rows] = part.astype(BF16)
        turned_ref[:, d * 128 : (d + 1) * 128] = m[:128].T


def far_kernel(*refs):
    *blocks, weight_ref, keys_ref, sent_ref = refs
    keys_ref[...] = raw_keys(blocks, weight_ref[...])
    sent_ref[...] = keys_ref[...].astype(BF16)


def turn_kernel(b0, b1, b3, b2, out_ref):
    for i, b in enumerate((b0, b1, b3, b2)):
        out_ref[:, i * 128 : (i + 1) * 128] = b[...].T


def far_gradient_kernel(turned_ref, first_ref, sides_ref, last_ref, rest_ref, out_ref):
    keys = (first_ref[...], sides_ref[:128], sides_ref[128:], last_ref[...])
    rests = (rest_ref[:128], rest_ref[128:256], rest_ref[384:512], rest_ref[256:384])
    residual = jnp.concatenate([(k + r.astype(F32)).astype(BF16) for k, r in zip(keys, rests)], axis=0)
    out_ref[...] = jnp.dot(turned_ref[...], residual, preferred_element_type=F32)


def near_gradient_kernel(turned_ref, part_ref, rest_ref, sides_ref, last_ref, far_ref, out_ref, squares_ref):
    rests = (rest_ref[512:], sides_ref[:128], last_ref[...], sides_ref[128:])
    rest = jnp.concatenate([r.astype(F32) for r in rests], axis=0)
    residual = (part_ref[...] + rest).astype(BF16)
    squares = jnp.zeros((8, COLS), F32)
    for x in range(NX):
        rows = slice(x * 512, (x + 1) * 512)
        near = jnp.dot(turned_ref[rows], residual, preferred_element_type=F32)
        gradient = (near + far_ref[rows]) * FACTOR
        out_ref[x, :512] = gradient.astype(BF16)
        out_ref[x, 512:] = jnp.zeros((16, COLS), BF16)
        squares += jnp.sum((gradient * gradient).reshape(64, 8, COLS), axis=0)
    squares_ref[...] = squares[:, :128] + squares[:, 128:]


def embed_kernel(squares_ref, _, out_ref):
    squares = squares_ref[...]
    high = squares.astype(BF16).astype(F32)
    middle = (squares - high).astype(BF16).astype(F32)
    low = squares - high - middle
    upper = jnp.concatenate([high, middle], axis=1)
    lower = jnp.concatenate([low, jnp.zeros((8, 128), F32)], axis=1)
    rows = jnp.concatenate([upper, lower], axis=0).astype(BF16)
    for x in range(NX):
        out_ref[x] = rows


def embed(squares, gradient):
    return pl.pallas_call(
        embed_kernel,
        grid=(1,),
        in_specs=[pl.BlockSpec((8, 128), lambda i: (0, 0)), pl.BlockSpec(memory_space=pl.ANY)],
        out_specs=pl.BlockSpec((NX, 16, COLS), lambda i: (0, 32, 0)),
        out_shape=SDS((NX, 528, COLS), BF16),
        input_output_aliases={1: 0},
        compiler_params=PARAMS,
        name="embed",
    )(squares, gradient)


def sum_kernel(blocks_ref, _, out_ref):
    out_ref[...] = jnp.sum(blocks_ref[...].astype(F32), axis=0)


def step_kernel(order_ref, squares_ref, rows_ref, weight_ref, global_ref, out_ref, new_ref):
    total = jnp.sum(squares_ref[...].astype(F32), axis=0)
    total = jnp.sum(total, axis=(0, 1), keepdims=True)
    rate = 0.25 * lax.rsqrt(total / (D * KV) + 1e-06)
    for x in range(NX):
        columns = slice(x * COLS, (x + 1) * COLS)
        weight = weight_ref[0, :, columns].astype(F32)
        new_ref[:, columns] = weight - rows_ref[x].astype(F32) * rate
    for slot in range(FRAG_HEADS):
        at = pl.ds(pl.multiple_of(order_ref[slot] * HEAD, HEAD), HEAD)
        incoming = global_ref[:, slot * HEAD : (slot + 1) * HEAD].astype(F32)
        new_ref[:, at] = 0.5 * new_ref[:, at] + 0.5 * incoming
    out_ref[0] = new_ref[...].astype(BF16)


def step(order, rows, weight, new_global):
    return pl.pallas_call(
        step_kernel,
        grid=(4,),
        in_specs=[
            SMEM,
            pl.BlockSpec((NX, 16, COLS), lambda i: (0, 32, 0)),
            pl.BlockSpec((NX, 128, COLS), lambda i: (0, i, 0)),
            pl.BlockSpec((1, 128, KV), lambda i: (0, i, 0)),
            pl.BlockSpec((128, COLS), lambda i: (i, 0)),
        ],
        out_specs=pl.BlockSpec((1, 128, KV), lambda i: (0, i, 0)),
        out_shape=SDS((1, 512, KV), BF16),
        scratch_shapes=[pltpu.VMEM((128, KV), F32)],
        compiler_params=PARAMS,
        name="step",
    )(order, rows, rows, weight, new_global)


def call(kernel, outs, *args, scalars=0, hbm=0, scratch=(), vmem_mib=16, out_space=pltpu.VMEM, flops=0):
    vmem = len(args) - scalars - hbm
    return pl.pallas_call(
        kernel,
        in_specs=[SMEM] * scalars
        + [pl.BlockSpec(memory_space=pltpu.VMEM)] * vmem
        + [pl.BlockSpec(memory_space=pltpu.HBM)] * hbm,
        scratch_shapes=scratch,
        out_specs=jax.tree.map(lambda _: pl.BlockSpec(memory_space=out_space), outs),
        out_shape=outs,
        compiler_params=pltpu.CompilerParams(vmem_limit_bytes=vmem_mib << 20),
        cost_estimate=pl.CostEstimate(flops=flops, bytes_accessed=4 << 20, transcendentals=0),
        name=kernel.__name__.removesuffix("_kernel"),
    )(*args)


def body(tokens, targets, local_weights, pending_delta, frag_order, global_frag, outer_momentum):
    index = lax.axis_index("fsdp").astype(jnp.int32).reshape(1)
    dot_flops = 2 * 512 * 2048 * COLS
    tall = (512, COLS)

    with jax.named_scope("activations"):
        other, *messages = call(
            pack_kernel,
            (SDS((128, 2048), BF16),) + (SDS((208, 2048), BF16),) * NX,
            index, tokens, local_weights, targets, scalars=1, hbm=3, out_space=pltpu.HBM, vmem_mib=58,
            scratch=[pltpu.VMEM(a.shape, BF16) for a in (tokens, local_weights, targets)]
            + [pltpu.VMEM((128, 2048), BF16)] * 2
            + [pltpu.VMEM((NX, 80, 2048), BF16), pltpu.SemaphoreType.DMA((3,)), pltpu.SemaphoreType.DMA((9,))],
        )
        arrived = flip(other, 1)
        near = rotate(messages)
        far = gather(arrived)

    with jax.named_scope("near_keys"):
        near_part, near_sent, columns, near_turned, first_keys = call(
            near_kernel,
            (SDS(tall, F32), SDS((640, COLS), BF16), SDS((2048, COLS), BF16), SDS((2048, 512), BF16), SDS((128, COLS), F32)),
            index, *near, arrived, scalars=1, flops=dot_flops,
        )
        rest = flip(near_sent, 1)

    with jax.named_scope("far_keys"):
        sides_keys, sides_sent = call(
            far_kernel, (SDS((256, COLS), F32), SDS((256, COLS), BF16)), far[1], far[3], columns, flops=dot_flops // 2
        )
        sides_rest = flip(sides_sent, 1)
        last_keys, last_sent = call(
            far_kernel, (SDS((128, COLS), F32), SDS((128, COLS), BF16)), far[2], columns, flops=dot_flops // 4
        )
        last_rest = flip(last_sent, 1)
        far_turned = call(turn_kernel, SDS((2048, 512), BF16), far[0], far[1], far[3], far[2])

    with jax.named_scope("gradient"):
        far_gradient = call(
            far_gradient_kernel, SDS((2048, COLS), F32),
            far_turned, first_keys, sides_keys, last_keys, rest, flops=dot_flops,
        )
        gradient, squares = call(
            near_gradient_kernel,
            (SDS((NX, 528, COLS), BF16), SDS((8, 128), F32)),
            near_turned, near_part, rest, sides_rest, last_rest, far_gradient, flops=dot_flops,
        )
        squares = squares + flip(squares, 1)
        embedded = embed(squares, gradient)
        by_rows = exchange(embedded, "fsdp", X_GROUPS)

    with jax.named_scope("outer_sum"):
        parts = exchange(pending_delta[0].reshape(64, 8, 256), "rep", None)
        total = call(sum_kernel, SDS((8, 256), F32), parts, arrived, hbm=1)
        rows = exchange(jnp.broadcast_to(total.astype(BF16)[None], (64, 8, 256)), "rep", None)
        mean = rows.astype(F32).reshape(512, 256) / lax.axis_size("rep")
        new_momentum = 0.9 * outer_momentum + mean
        new_global = (global_frag.astype(F32) - 0.7 * (mean + 0.9 * new_momentum)).astype(BF16)

    with jax.named_scope("step"):
        new_weights = step(frag_order, by_rows, local_weights, new_global)
    return (new_weights, new_global, new_momentum)


def solution(mesh):
    placed = (
        P(("rep", "fsdp"), None),
        P(("rep", "fsdp"), None),
        P("rep", "fsdp", None),
        P("rep", "fsdp", None),
        P(),
        P("fsdp", None),
        P("fsdp", None),
    )
    return jax.shard_map(
        body,
        mesh=mesh,
        in_specs=placed,
        out_specs=(P("rep", "fsdp", None), P("fsdp", None), P("fsdp", None)),
        check_vma=False,
    )
```

```python
import math

import jax
import jax.numpy as jnp
from jax import lax
from jax.experimental import pallas as pl
from jax.experimental.pallas import tpu as pltpu
from jax.sharding import PartitionSpec as P

D = 4096
HEAD = 128
FRAG_HEADS = 2
KV = 1024
NX = 4
COLS = KV // NX
FACTOR = 1.0 / math.sqrt(D)
F32 = jnp.float32
BF16 = jnp.bfloat16
SDS = jax.ShapeDtypeStruct
SMEM = pl.BlockSpec(memory_space=pltpu.SMEM)
PARAMS = pltpu.CompilerParams(vmem_limit_bytes=16 * 1024 * 1024)

X_GROUPS = [[x * 2 + h for x in range(NX)] for h in range(2)]


def exchange(blocks, axis, groups):
    return lax.all_to_all(blocks, axis, 0, 0, axis_index_groups=groups, tiled=True)


def flip(block, mask):
    return lax.ppermute(block, "fsdp", [(i, i ^ mask) for i in range(8)])


def rotate(blocks):
    moves = [[(x * 2 + h, (x + d) % NX * 2 + h) for x in range(NX) for h in range(2)] for d in range(NX)]
    return [blocks[0]] + [lax.ppermute(blocks[d], "fsdp", moves[d]) for d in (1, 2, 3)]


def gather(block):
    return rotate([block] * NX)


def pack_kernel(index_ref, *refs):
    sources, outs, held, (mine_ref, away_ref, columns_ref), (fetched, stored) = refs[:3], refs[3:8], refs[8:11], refs[11:14], refs[14:]
    fetches = [pltpu.make_async_copy(s, h, fetched.at[i]) for i, (s, h) in enumerate(zip(sources, held))]
    for fetch in fetches:
        fetch.start()
    half, x = lax.rem(index_ref[0], 2), lax.div(index_ref[0], 2)
    tokens_ref, weight_ref, targets_ref = held
    fetches[0].wait()
    floated = tokens_ref[...].astype(F32)
    scale = lax.rsqrt(jnp.mean(floated * floated, axis=-1, keepdims=True) + 1e-06)
    for ref, side in ((away_ref, 1 - half), (mine_ref, half)):
        for block in range(NX):
            start = pl.multiple_of((2 * block + side) * 512, 512)
            piece = tokens_ref[:, pl.ds(start, 512)].astype(F32) * scale
            ref[:, block * 512 : (block + 1) * 512] = piece.astype(BF16)
    stores = [pltpu.make_async_copy(away_ref, outs[0], stored.at[0])]
    stores += [pltpu.make_async_copy(mine_ref, out.at[:128], stored.at[1 + d]) for d, out in enumerate(outs[1:])]
    for store in stores:
        store.start()
    fetches[1].wait()
    fetches[2].wait()
    for d, out in enumerate(outs[1:]):
        columns = pl.ds(pl.multiple_of(lax.rem(x + d, NX) * COLS, COLS), COLS)
        for j in range(8):
            lanes = slice(j * COLS, (j + 1) * COLS)
            columns_ref[d, :64, lanes] = weight_ref[0, j * 64 : (j + 1) * 64, columns]
            columns_ref[d, 64:, lanes] = targets_ref[j * 16 : (j + 1) * 16, columns]
        store = pltpu.make_async_copy(columns_ref.at[d], out.at[128:], stored.at[5 + d])
        store.start()
        stores.append(store)
    for store in stores:
        store.wait()


def raw_keys(blocks, weight):
    lhs = jnp.concatenate([b[:128] for b in blocks], axis=0)
    return jnp.dot(lhs, weight, preferred_element_type=F32) * FACTOR


def near_kernel(index_ref, m0, m1, m2, m3, arrived_ref, part_ref, sent_ref, weight_ref, turned_ref, first_ref):
    messages = (m0, m1, m2, m3)
    for d, m in enumerate(messages):
        source = lax.rem(lax.div(index_ref[0], 2) - d + NX, NX)
        for j in range(8):
            rows = pl.ds(pl.multiple_of(source * 512 + j * 64, 64), 64)
            weight_ref[rows, :] = m[128:192, j * COLS : (j + 1) * COLS]
    keys = raw_keys((*messages, arrived_ref), weight_ref[...])
    first_ref[...] = keys[512:]
    sent_ref[512:] = keys[512:].astype(BF16)
    for d, m in enumerate(messages):
        for j in range(8):
            rows = slice(d * 128 + j * 16, d * 128 + (j + 1) * 16)
            part = keys[rows] - m[192:, j * COLS : (j + 1) * COLS].astype(F32)
            part_ref[rows] = part
            sent_ref[rows] = part.astype(BF16)
        turned_ref[:, d * 128 : (d + 1) * 128] = m[:128].T


def far_kernel(*refs):
    *blocks, weight_ref, keys_ref, sent_ref = refs
    keys_ref[...] = raw_keys(blocks, weight_ref[...])
    sent_ref[...] = keys_ref[...].astype(BF16)


def turn_kernel(b0, b1, b3, b2, out_ref):
    for i, b in enumerate((b0, b1, b3, b2)):
        out_ref[:, i * 128 : (i + 1) * 128] = b[...].T


def far_gradient_kernel(turned_ref, first_ref, sides_ref, last_ref, rest_ref, out_ref):
    keys = (first_ref[...], sides_ref[:128], sides_ref[128:], last_ref[...])
    rests = (rest_ref[:128], rest_ref[128:256], rest_ref[384:512], rest_ref[256:384])
    residual = jnp.concatenate([(k + r.astype(F32)).astype(BF16) for k, r in zip(keys, rests)], axis=0)
    out_ref[...] = jnp.dot(turned_ref[...], residual, preferred_element_type=F32)


def near_gradient_kernel(turned_ref, part_ref, rest_ref, sides_ref, last_ref, far_ref, out_ref, squares_ref):
    rests = (rest_ref[512:], sides_ref[:128], last_ref[...], sides_ref[128:])
    rest = jnp.concatenate([r.astype(F32) for r in rests], axis=0)
    residual = (part_ref[...] + rest).astype(BF16)
    squares = jnp.zeros((8, COLS), F32)
    for x in range(NX):
        rows = slice(x * 512, (x + 1) * 512)
        near = jnp.dot(turned_ref[rows], residual, preferred_element_type=F32)
        gradient = (near + far_ref[rows]) * FACTOR
        out_ref[x, :512] = gradient.astype(BF16)
        squares += jnp.sum((gradient * gradient).reshape(64, 8, COLS), axis=0)
    squares = squares[:, :128] + squares[:, 128:]
    squares_ref[...] = squares
    high = squares.astype(BF16).astype(F32)
    middle = (squares - high).astype(BF16).astype(F32)
    low = squares - high - middle
    upper = jnp.concatenate([high, middle], axis=1)
    lower = jnp.concatenate([low, jnp.zeros((8, 128), F32)], axis=1)
    rows = jnp.concatenate([upper, lower], axis=0).astype(BF16)
    for x in range(NX):
        out_ref[x, 512:] = rows


def sum_kernel(blocks_ref, _, out_ref):
    out_ref[...] = jnp.sum(blocks_ref[...].astype(F32), axis=0)


def step_kernel(order_ref, squares_ref, rows_ref, weight_ref, global_ref, s0, s1, s2, s3, out_ref):
    total = jnp.sum(squares_ref[...].astype(F32), axis=0)
    total = jnp.sum(total, axis=(0, 1), keepdims=True)
    total += jnp.sum(s0[...] + s1[...] + s2[...] + s3[...], axis=(0, 1), keepdims=True)
    rate = 0.25 * lax.rsqrt(total / (D * KV) + 1e-06)
    for x in range(NX):
        columns = slice(x * COLS, (x + 1) * COLS)
        stepped = weight_ref[0, :, columns].astype(F32) - rows_ref[x].astype(F32) * rate
        out_ref[0, :, columns] = stepped.astype(BF16)
    for slot in range(FRAG_HEADS):
        head = order_ref[slot]
        at = pl.ds(pl.multiple_of(head * HEAD, HEAD), HEAD)
        inner = pl.ds(pl.multiple_of(lax.rem(head, 2) * HEAD, HEAD), HEAD)
        gradient = rows_ref[lax.div(head, 2), :, inner].astype(F32)
        stepped = weight_ref[0, :, at].astype(F32) - gradient * rate
        incoming = global_ref[:, slot * HEAD : (slot + 1) * HEAD].astype(F32)
        out_ref[0, :, at] = (0.5 * stepped + 0.5 * incoming).astype(BF16)


def step(order, rows, weight, new_global, others):
    return pl.pallas_call(
        step_kernel,
        grid=(4,),
        in_specs=[
            SMEM,
            pl.BlockSpec((NX, 16, COLS), lambda i: (0, 32, 0)),
            pl.BlockSpec((NX, 128, COLS), lambda i: (0, i, 0)),
            pl.BlockSpec((1, 128, KV), lambda i: (0, i, 0)),
            pl.BlockSpec((128, COLS), lambda i: (i, 0)),
        ]
        + [pl.BlockSpec((8, 128), lambda i: (0, 0))] * NX,
        out_specs=pl.BlockSpec((1, 128, KV), lambda i: (0, i, 0)),
        out_shape=SDS((1, 512, KV), BF16),
        compiler_params=PARAMS,
        name="step",
    )(order, rows, rows, weight, new_global, *others)


def call(kernel, outs, *args, scalars=0, hbm=0, scratch=(), vmem_mib=16, out_space=pltpu.VMEM, flops=0):
    vmem = len(args) - scalars - hbm
    return pl.pallas_call(
        kernel,
        in_specs=[SMEM] * scalars
        + [pl.BlockSpec(memory_space=pltpu.VMEM)] * vmem
        + [pl.BlockSpec(memory_space=pltpu.HBM)] * hbm,
        scratch_shapes=scratch,
        out_specs=jax.tree.map(lambda _: pl.BlockSpec(memory_space=out_space), outs),
        out_shape=outs,
        compiler_params=pltpu.CompilerParams(vmem_limit_bytes=vmem_mib << 20),
        cost_estimate=pl.CostEstimate(flops=flops, bytes_accessed=4 << 20, transcendentals=0),
        name=kernel.__name__.removesuffix("_kernel"),
    )(*args)


def body(tokens, targets, local_weights, pending_delta, frag_order, global_frag, outer_momentum):
    index = lax.axis_index("fsdp").astype(jnp.int32).reshape(1)
    dot_flops = 2 * 512 * 2048 * COLS
    tall = (512, COLS)

    with jax.named_scope("activations"):
        other, *messages = call(
            pack_kernel,
            (SDS((128, 2048), BF16),) + (SDS((208, 2048), BF16),) * NX,
            index, tokens, local_weights, targets, scalars=1, hbm=3, out_space=pltpu.HBM, vmem_mib=58,
            scratch=[pltpu.VMEM(a.shape, BF16) for a in (tokens, local_weights, targets)]
            + [pltpu.VMEM((128, 2048), BF16)] * 2
            + [pltpu.VMEM((NX, 80, 2048), BF16), pltpu.SemaphoreType.DMA((3,)), pltpu.SemaphoreType.DMA((9,))],
        )
        arrived = flip(other, 1)
        near = rotate(messages)
        far = gather(arrived)

    with jax.named_scope("near_keys"):
        near_part, near_sent, columns, near_turned, first_keys = call(
            near_kernel,
            (SDS(tall, F32), SDS((640, COLS), BF16), SDS((2048, COLS), BF16), SDS((2048, 512), BF16), SDS((128, COLS), F32)),
            index, *near, arrived, scalars=1, flops=dot_flops,
        )
        rest = flip(near_sent, 1)

    with jax.named_scope("far_keys"):
        sides_keys, sides_sent = call(
            far_kernel, (SDS((256, COLS), F32), SDS((256, COLS), BF16)), far[1], far[3], columns, flops=dot_flops // 2
        )
        sides_rest = flip(sides_sent, 1)
        last_keys, last_sent = call(
            far_kernel, (SDS((128, COLS), F32), SDS((128, COLS), BF16)), far[2], columns, flops=dot_flops // 4
        )
        last_rest = flip(last_sent, 1)
        far_turned = call(turn_kernel, SDS((2048, 512), BF16), far[0], far[1], far[3], far[2])

    with jax.named_scope("gradient"):
        far_gradient = call(
            far_gradient_kernel, SDS((2048, COLS), F32),
            far_turned, first_keys, sides_keys, last_keys, rest, flops=dot_flops,
        )
        gradient, squares = call(
            near_gradient_kernel,
            (SDS((NX, 528, COLS), BF16), SDS((8, 128), F32)),
            near_turned, near_part, rest, sides_rest, last_rest, far_gradient, flops=dot_flops,
        )
        by_rows = exchange(gradient, "fsdp", X_GROUPS)
        crossings = [[(x * 2 + h, (x + d) % NX * 2 + 1 - h) for x in range(NX) for h in range(2)] for d in range(NX)]
        others = [lax.ppermute(squares, "fsdp", crossing) for crossing in crossings]

    with jax.named_scope("outer_sum"):
        parts = exchange(pending_delta[0].reshape(64, 8, 256), "rep", None)
        total = call(sum_kernel, SDS((8, 256), F32), parts, arrived, hbm=1)
        rows = exchange(jnp.broadcast_to(total.astype(BF16)[None], (64, 8, 256)), "rep", None)
        mean = rows.astype(F32).reshape(512, 256) / lax.axis_size("rep")
        new_momentum = 0.9 * outer_momentum + mean
        new_global = (global_frag.astype(F32) - 0.7 * (mean + 0.9 * new_momentum)).astype(BF16)

    with jax.named_scope("step"):
        new_weights = step(frag_order, by_rows, local_weights, new_global, others)
    return (new_weights, new_global, new_momentum)


def solution(mesh):
    placed = (
        P(("rep", "fsdp"), None),
        P(("rep", "fsdp"), None),
        P("rep", "fsdp", None),
        P("rep", "fsdp", None),
        P(),
        P("fsdp", None),
        P("fsdp", None),
    )
    return jax.shard_map(
        body,
        mesh=mesh,
        in_specs=placed,
        out_specs=(P("rep", "fsdp", None), P("fsdp", None), P("fsdp", None)),
        check_vma=False,
    )
```

```python
import math

import jax
import jax.numpy as jnp
from jax import lax
from jax.experimental import pallas as pl
from jax.experimental.pallas import tpu as pltpu
from jax.sharding import PartitionSpec as P

D = 4096
HEAD = 128
FRAG_HEADS = 2
KV = 1024
NX = 4
COLS = KV // NX
FACTOR = 1.0 / math.sqrt(D)
F32 = jnp.float32
BF16 = jnp.bfloat16
SDS = jax.ShapeDtypeStruct
SMEM = pl.BlockSpec(memory_space=pltpu.SMEM)
PARAMS = pltpu.CompilerParams(vmem_limit_bytes=16 * 1024 * 1024)

X_GROUPS = [[x * 2 + h for x in range(NX)] for h in range(2)]


def exchange(blocks, axis, groups):
    return lax.all_to_all(blocks, axis, 0, 0, axis_index_groups=groups, tiled=True)


def flip(block, mask):
    return lax.ppermute(block, "fsdp", [(i, i ^ mask) for i in range(8)])


def rotate(blocks):
    moves = [[(x * 2 + h, (x + d) % NX * 2 + h) for x in range(NX) for h in range(2)] for d in range(NX)]
    return [blocks[0]] + [lax.ppermute(blocks[d], "fsdp", moves[d]) for d in (1, 2, 3)]


def gather(block):
    return rotate([block] * NX)


def pack_kernel(index_ref, *refs):
    sources, outs, held, (mine_ref, away_ref, columns_ref), (fetched, stored) = refs[:3], refs[3:8], refs[8:11], refs[11:14], refs[14:]
    fetches = [pltpu.make_async_copy(s, h, fetched.at[i]) for i, (s, h) in enumerate(zip(sources, held))]
    for fetch in fetches:
        fetch.start()
    half, x = lax.rem(index_ref[0], 2), lax.div(index_ref[0], 2)
    tokens_ref, weight_ref, targets_ref = held
    fetches[0].wait()
    floated = tokens_ref[...].astype(F32)
    scale = lax.rsqrt(jnp.mean(floated * floated, axis=-1, keepdims=True) + 1e-06)
    for ref, side in ((away_ref, 1 - half), (mine_ref, half)):
        for block in range(NX):
            start = pl.multiple_of((2 * block + side) * 512, 512)
            piece = tokens_ref[:, pl.ds(start, 512)].astype(F32) * scale
            ref[:, block * 512 : (block + 1) * 512] = piece.astype(BF16)
    stores = [pltpu.make_async_copy(away_ref, outs[0], stored.at[0])]
    stores += [pltpu.make_async_copy(mine_ref, out.at[:128], stored.at[1 + d]) for d, out in enumerate(outs[1:])]
    for store in stores:
        store.start()
    fetches[1].wait()
    fetches[2].wait()
    for d, out in enumerate(outs[1:]):
        columns = pl.ds(pl.multiple_of(lax.rem(x + d, NX) * COLS, COLS), COLS)
        for j in range(8):
            lanes = slice(j * COLS, (j + 1) * COLS)
            columns_ref[d, :64, lanes] = weight_ref[0, j * 64 : (j + 1) * 64, columns]
            columns_ref[d, 64:, lanes] = targets_ref[j * 16 : (j + 1) * 16, columns]
        store = pltpu.make_async_copy(columns_ref.at[d], out.at[128:], stored.at[5 + d])
        store.start()
        stores.append(store)
    for store in stores:
        store.wait()


def raw_keys(blocks, weight):
    lhs = jnp.concatenate([b[:128] for b in blocks], axis=0)
    return jnp.dot(lhs, weight, preferred_element_type=F32) * FACTOR


def near_kernel(index_ref, m0, m1, m2, m3, arrived_ref, part_ref, sent_ref, weight_ref, turned_ref, first_ref):
    messages = (m0, m1, m2, m3)
    for d, m in enumerate(messages):
        source = lax.rem(lax.div(index_ref[0], 2) - d + NX, NX)
        for j in range(8):
            rows = pl.ds(pl.multiple_of(source * 512 + j * 64, 64), 64)
            weight_ref[rows, :] = m[128:192, j * COLS : (j + 1) * COLS]
    keys = raw_keys((*messages, arrived_ref), weight_ref[...])
    first_ref[...] = keys[512:]
    sent_ref[512:] = keys[512:].astype(BF16)
    for d, m in enumerate(messages):
        for j in range(8):
            rows = slice(d * 128 + j * 16, d * 128 + (j + 1) * 16)
            part = keys[rows] - m[192:, j * COLS : (j + 1) * COLS].astype(F32)
            part_ref[rows] = part
            sent_ref[rows] = part.astype(BF16)
        turned_ref[:, d * 128 : (d + 1) * 128] = m[:128].T


def far_kernel(*refs):
    *blocks, weight_ref, keys_ref, sent_ref = refs
    keys_ref[...] = raw_keys(blocks, weight_ref[...])
    sent_ref[...] = keys_ref[...].astype(BF16)


def turn_kernel(b0, b1, b3, b2, out_ref):
    for i, b in enumerate((b0, b1, b3, b2)):
        out_ref[:, i * 128 : (i + 1) * 128] = b[...].T


def far_gradient_kernel(turned_ref, first_ref, sides_ref, last_ref, rest_ref, out_ref):
    keys = (first_ref[...], sides_ref[:128], sides_ref[128:], last_ref[...])
    rests = (rest_ref[:128], rest_ref[128:256], rest_ref[384:512], rest_ref[256:384])
    residual = jnp.concatenate([(k + r.astype(F32)).astype(BF16) for k, r in zip(keys, rests)], axis=0)
    out_ref[...] = jnp.dot(turned_ref[...], residual, preferred_element_type=F32)


def near_gradient_kernel(turned_ref, part_ref, rest_ref, sides_ref, last_ref, far_ref, out_ref, squares_ref):
    rests = (rest_ref[512:], sides_ref[:128], last_ref[...], sides_ref[128:])
    rest = jnp.concatenate([r.astype(F32) for r in rests], axis=0)
    residual = (part_ref[...] + rest).astype(BF16)
    squares = jnp.zeros((8, COLS), F32)
    for x in range(NX):
        rows = slice(x * 512, (x + 1) * 512)
        near = jnp.dot(turned_ref[rows], residual, preferred_element_type=F32)
        gradient = (near + far_ref[rows]) * FACTOR
        out_ref[x, :512] = gradient.astype(BF16)
        out_ref[x, 512:] = jnp.zeros((16, COLS), BF16)
        squares += jnp.sum((gradient * gradient).reshape(64, 8, COLS), axis=0)
    squares_ref[...] = squares[:, :128] + squares[:, 128:]


def embed_kernel(squares_ref, _, out_ref):
    squares = squares_ref[...]
    high = squares.astype(BF16).astype(F32)
    middle = (squares - high).astype(BF16).astype(F32)
    low = squares - high - middle
    upper = jnp.concatenate([high, middle], axis=1)
    lower = jnp.concatenate([low, jnp.zeros((8, 128), F32)], axis=1)
    rows = jnp.concatenate([upper, lower], axis=0).astype(BF16)
    for x in range(NX):
        out_ref[x] = rows


def embed(squares, gradient):
    return pl.pallas_call(
        embed_kernel,
        grid=(1,),
        in_specs=[pl.BlockSpec((8, 128), lambda i: (0, 0)), pl.BlockSpec(memory_space=pl.ANY)],
        out_specs=pl.BlockSpec((NX, 16, COLS), lambda i: (0, 32, 0)),
        out_shape=SDS((NX, 528, COLS), BF16),
        input_output_aliases={1: 0},
        compiler_params=PARAMS,
        name="embed",
    )(squares, gradient)


def sum_kernel(blocks_ref, _, out_ref):
    out_ref[...] = jnp.sum(blocks_ref[...].astype(F32), axis=0)


def step_kernel(order_ref, squares_ref, rows_ref, weight_ref, global_ref, out_ref, new_ref):
    total = jnp.sum(squares_ref[...].astype(F32), axis=0)
    total = jnp.sum(total, axis=(0, 1), keepdims=True)
    rate = 0.25 * lax.rsqrt(total / (D * KV) + 1e-06)
    for x in range(NX):
        columns = slice(x * COLS, (x + 1) * COLS)
        weight = weight_ref[0, :, columns].astype(F32)
        new_ref[:, columns] = weight - rows_ref[x].astype(F32) * rate
    for slot in range(FRAG_HEADS):
        at = pl.ds(pl.multiple_of(order_ref[slot] * HEAD, HEAD), HEAD)
        incoming = global_ref[:, slot * HEAD : (slot + 1) * HEAD].astype(F32)
        new_ref[:, at] = 0.5 * new_ref[:, at] + 0.5 * incoming
    out_ref[0] = new_ref[...].astype(BF16)


def step(order, rows, weight, new_global):
    return pl.pallas_call(
        step_kernel,
        grid=(4,),
        in_specs=[
            SMEM,
            pl.BlockSpec((NX, 16, COLS), lambda i: (0, 32, 0)),
            pl.BlockSpec((NX, 128, COLS), lambda i: (0, i, 0)),
            pl.BlockSpec((1, 128, KV), lambda i: (0, i, 0)),
            pl.BlockSpec((128, COLS), lambda i: (i, 0)),
        ],
        out_specs=pl.BlockSpec((1, 128, KV), lambda i: (0, i, 0)),
        out_shape=SDS((1, 512, KV), BF16),
        scratch_shapes=[pltpu.VMEM((128, KV), F32)],
        compiler_params=PARAMS,
        name="step",
    )(order, rows, rows, weight, new_global)


def call(kernel, outs, *args, scalars=0, hbm=0, scratch=(), vmem_mib=16, out_space=pltpu.VMEM, flops=0):
    vmem = len(args) - scalars - hbm
    return pl.pallas_call(
        kernel,
        in_specs=[SMEM] * scalars
        + [pl.BlockSpec(memory_space=pltpu.VMEM)] * vmem
        + [pl.BlockSpec(memory_space=pltpu.HBM)] * hbm,
        scratch_shapes=scratch,
        out_specs=jax.tree.map(lambda _: pl.BlockSpec(memory_space=out_space), outs),
        out_shape=outs,
        compiler_params=pltpu.CompilerParams(vmem_limit_bytes=vmem_mib << 20),
        cost_estimate=pl.CostEstimate(flops=flops, bytes_accessed=4 << 20, transcendentals=0),
        name=kernel.__name__.removesuffix("_kernel"),
    )(*args)


def body(tokens, targets, local_weights, pending_delta, frag_order, global_frag, outer_momentum):
    index = lax.axis_index("fsdp").astype(jnp.int32).reshape(1)
    dot_flops = 2 * 512 * 2048 * COLS
    tall = (512, COLS)

    with jax.named_scope("activations"):
        other, *messages = call(
            pack_kernel,
            (SDS((128, 2048), BF16),) + (SDS((208, 2048), BF16),) * NX,
            index, tokens, local_weights, targets, scalars=1, hbm=3, out_space=pltpu.HBM, vmem_mib=58,
            scratch=[pltpu.VMEM(a.shape, BF16) for a in (tokens, local_weights, targets)]
            + [pltpu.VMEM((128, 2048), BF16)] * 2
            + [pltpu.VMEM((NX, 80, 2048), BF16), pltpu.SemaphoreType.DMA((3,)), pltpu.SemaphoreType.DMA((9,))],
        )
        arrived = flip(other, 1)
        near = rotate(messages)
        far = gather(arrived)

    with jax.named_scope("near_keys"):
        near_part, near_sent, columns, near_turned, first_keys = call(
            near_kernel,
            (SDS(tall, F32), SDS((640, COLS), BF16), SDS((2048, COLS), BF16), SDS((2048, 512), BF16), SDS((128, COLS), F32)),
            index, *near, arrived, scalars=1, flops=dot_flops,
        )
        rest = flip(near_sent, 1)

    with jax.named_scope("far_keys"):
        sides_keys, sides_sent = call(
            far_kernel, (SDS((256, COLS), F32), SDS((256, COLS), BF16)), far[1], far[3], columns, flops=dot_flops // 2
        )
        sides_rest = flip(sides_sent, 1)
        last_keys, last_sent = call(
            far_kernel, (SDS((128, COLS), F32), SDS((128, COLS), BF16)), far[2], columns, flops=dot_flops // 4
        )
        last_rest = flip(last_sent, 1)
        far_turned = call(turn_kernel, SDS((2048, 512), BF16), far[0], far[1], far[3], far[2])

    with jax.named_scope("gradient"):
        far_gradient = call(
            far_gradient_kernel, SDS((2048, COLS), F32),
            far_turned, first_keys, sides_keys, last_keys, rest, flops=dot_flops,
        )
        gradient, squares = call(
            near_gradient_kernel,
            (SDS((NX, 528, COLS), BF16), SDS((8, 128), F32)),
            near_turned, near_part, rest, sides_rest, last_rest, far_gradient, flops=dot_flops,
        )
        squares = squares + flip(squares, 1)
        embedded = embed(squares, gradient)
        by_rows = exchange(embedded, "fsdp", X_GROUPS)

    with jax.named_scope("outer_sum"):
        parts = exchange(pending_delta[0].reshape(64, 8, 256), "rep", None)
        total = call(sum_kernel, SDS((8, 256), F32), parts, arrived, hbm=1, flops=6 * 10**9)
        rows = exchange(jnp.broadcast_to(total.astype(BF16)[None], (64, 8, 256)), "rep", None)
        mean = rows.astype(F32).reshape(512, 256) / lax.axis_size("rep")
        new_momentum = 0.9 * outer_momentum + mean
        new_global = (global_frag.astype(F32) - 0.7 * (mean + 0.9 * new_momentum)).astype(BF16)

    with jax.named_scope("step"):
        new_weights = step(frag_order, by_rows, local_weights, new_global)
    return (new_weights, new_global, new_momentum)


def solution(mesh):
    placed = (
        P(("rep", "fsdp"), None),
        P(("rep", "fsdp"), None),
        P("rep", "fsdp", None),
        P("rep", "fsdp", None),
        P(),
        P("fsdp", None),
        P("fsdp", None),
    )
    return jax.shard_map(
        body,
        mesh=mesh,
        in_specs=placed,
        out_specs=(P("rep", "fsdp", None), P("fsdp", None), P("fsdp", None)),
        check_vma=False,
    )
```
